256 devices in a mesh: section: 4 (over y), ctx: 64 (over x, z, core).
Axes of the slice: x: 4, y: 4, z: 8, core: 2. Of those that a mesh axis runs over, the one named last changes fastest.
Arguments:
- section_in: bfloat16 [4, 16384, 4096], P('section', 'ctx'), may hold values from -6 to 6
- proj_weight: bfloat16 [4, 4096, 256], P('section'), may hold values from -0.09375 to 0.09375
- conv_weight: bfloat16 [4, 4, 4352], P('section'), may hold values from -3 to 3
- log_decay: float32 [4, 16384, 64], P('section', 'ctx'), as said below
- step_size: float32 [4, 16384, 64], P('section', 'ctx'), may hold values from 0.5 to 2
- skip_gain: float32 [4, 64], P('section'), may hold values from 1 to 10
- norm_gain: bfloat16 [4, 4096], P('section'), may hold values from 0.5 to 1.5
- carry_state: float32 [4, 64, 128, 64], P('section'), may hold values from -192 to 192
- carry_rows: bfloat16 [4, 3, 4352], P('section'), may hold values from -6 to 6
Outputs:
- handed_rows: bfloat16 [4, 16384, 4096], P('section', 'ctx')
The draws below stay inside these ranges and needn't reach their ends.
Inputs may be any that keep to these rules, and one draw needn't show every extreme that they name: `log_decay`: every entry is negative.
All inputs are finite; a program needn't handle non-finite values.
Results may differ from the reference program's by a relative error of at most 0.004.
Values may be sent and summed in bfloat16 or wider, within the bound.
No kernel may reach another device: no remote copies, remote signals or barrier semaphores. Data moves between devices by JAX's collectives and lax.ppermute only.
A program may use at most 320 MiB of HBM per device.

```python
import math
import jax
import jax.numpy as jnp
from jax import lax

HEAD_COUNT = 64
HEAD_DIM = 64
STATE = 128
CONV = 4
GROUP = 256
TOK_DEV = 256
CHANNELS = 4096
SEGMENT_TOKENS = 16384
SECTION_COUNT = 4


def draw_log_decay(key, part):
    key_vectors = jax.random.split(jax.random.fold_in(key, 11), 7)
    share = 0.5
    slow_heads = jax.random.uniform(key_vectors[0], (SECTION_COUNT, HEAD_COUNT)) < share
    fast_rate = jnp.exp(jax.random.uniform(key_vectors[1], (SECTION_COUNT, HEAD_COUNT), minval=jnp.log(1.0 / 50.0), maxval=jnp.log(1.0 / 30.0)))
    slow_rate = jnp.exp(jax.random.uniform(key_vectors[2], (SECTION_COUNT, HEAD_COUNT), minval=jnp.log(0.05), maxval=jnp.log(0.3))) / SEGMENT_TOKENS
    head_decay_rate = jnp.where(slow_heads, slow_rate, fast_rate)
    jaggedness = jax.random.uniform(key_vectors[3], (SECTION_COUNT, SEGMENT_TOKENS, HEAD_COUNT), minval=0.5, maxval=2.0)
    device_multiplier = jnp.exp(jax.random.uniform(key_vectors[4], (SECTION_COUNT, SEGMENT_TOKENS // TOK_DEV, HEAD_COUNT), minval=jnp.log(0.5), maxval=jnp.log(2.0)))
    device_multiplier = jnp.repeat(device_multiplier, TOK_DEV, axis=1)
    spike_positions = jax.random.randint(key_vectors[5], (SECTION_COUNT, 3), 0, SEGMENT_TOKENS)
    spike_rows = jnp.any(jnp.arange(SEGMENT_TOKENS)[None, None, :] == spike_positions[:, :, None], axis=1).astype(jnp.float32)
    spike_loss = jax.random.uniform(key_vectors[6], (SECTION_COUNT, SEGMENT_TOKENS, HEAD_COUNT), minval=0.22, maxval=0.69)
    return -(head_decay_rate[:, None, :] * jaggedness * device_multiplier + spike_rows[:, :, None] * spike_loss)


def steps_of(key, dims, pieces, smallest, high):
    gain, own = 1.0, jax.random.fold_in(key, 6)
    for position, shards_of in pieces:
        heights = jnp.exp(jax.random.uniform(jax.random.fold_in(own, position), (shards_of,), jnp.float32, smallest / len(pieces), high / len(pieces)))
        gain = gain * jnp.repeat(heights, dims[position] // shards_of).reshape([-1 if axis == position else 1 for axis in range(len(dims))])
    return gain


def noise(rng, extent, scale, most, cuts=(), held_as=jnp.bfloat16):
    result = scale * jax.random.normal(rng, extent, jnp.float32)
    if cuts:
        result = result * steps_of(rng, extent, cuts, -0.22, 0.18)
    return jnp.clip(result, -most, most).astype(held_as)


def setup_inputs(seed: int = 0) -> dict:
    keys = jax.random.split(jax.random.key(seed), 10)
    return {
        "section_in": noise(keys[0], (SECTION_COUNT, SEGMENT_TOKENS, CHANNELS), 1.0, 6.0, ((0, 4), (1, 64))),
        "proj_weight": noise(keys[1], (SECTION_COUNT, CHANNELS, 2 * STATE), CHANNELS ** -0.5, 0.09375, ((0, 4),)),
        "conv_weight": noise(keys[2], (SECTION_COUNT, CONV, CHANNELS + 2 * STATE), 0.5, 3.0, ((0, 4),)),
        "log_decay": draw_log_decay(jax.random.fold_in(keys[9], 71), 0),
        "step_size": jnp.clip(jnp.exp(math.log(2.0) - 1.3862944 * jax.random.uniform(keys[4], (SECTION_COUNT, SEGMENT_TOKENS, HEAD_COUNT), jnp.float32) ** steps_of(keys[4], (SECTION_COUNT, SEGMENT_TOKENS, HEAD_COUNT), ((0, 4), (1, 64)), -0.2, 0.2)), 0.5, 2.0),
        "skip_gain": jnp.clip(jnp.exp(math.log(10.0) - 2.3025851 * jax.random.uniform(keys[5], (SECTION_COUNT, HEAD_COUNT), jnp.float32) ** steps_of(keys[5], (SECTION_COUNT, HEAD_COUNT), ((0, 4),), -0.2, 0.2)), 1.0, 10.0),
        "norm_gain": jnp.clip(1.0 + 0.1 * jax.random.normal(keys[6], (SECTION_COUNT, CHANNELS), jnp.float32), 0.5, 1.5).astype(jnp.bfloat16),
        "carry_state": noise(keys[7], (SECTION_COUNT, HEAD_COUNT, STATE, HEAD_DIM), (0.25 * SEGMENT_TOKENS ** 0.5), 192.0, ((0, 4),), jnp.float32),
        "carry_rows": noise(keys[8], (SECTION_COUNT, CONV - 1, CHANNELS + 2 * STATE), 1.0, 6.0, ((0, 4),)),
    }


def mamba_layer(current, projection, conv_taps, log_rates, step_rows, skip_term, gain_row, start_state, start_rows):
    tokens = current.shape[0]
    channels = current.shape[1]
    blocks = tokens // GROUP
    projected = jnp.dot(current, projection, preferred_element_type=jnp.float32).astype(jnp.bfloat16)
    wide_rows = jnp.concatenate([current, projected], axis=1)
    padded = jnp.concatenate([start_rows, wide_rows], axis=0)
    conv_sum = jnp.zeros(wide_rows.shape, jnp.float32)
    for tap_id in range(CONV):
        conv_sum = conv_sum + conv_taps[tap_id].astype(jnp.float32) * padded[tap_id:tap_id + tokens].astype(jnp.float32)
    activated = jax.nn.silu(conv_sum).astype(jnp.bfloat16)
    values = activated[:, :channels].reshape(blocks, GROUP, HEAD_COUNT, HEAD_DIM)
    keys_in = activated[:, channels:channels + STATE].reshape(blocks, GROUP, STATE)
    queries = activated[:, channels + STATE:].reshape(blocks, GROUP, STATE)
    rate_blocks = log_rates.reshape(blocks, GROUP, HEAD_COUNT)
    step_blocks = step_rows.reshape(blocks, GROUP, HEAD_COUNT)
    causal_mask = jnp.tril(jnp.ones((GROUP, GROUP), jnp.bool_))[:, :, None]
    highest = lax.Precision.HIGHEST

    def one_block(carry_now, inputs):
        block_vals, block_keys, block_queries, block_rates, block_steps = inputs
        cumulative = jnp.cumsum(block_rates, axis=0)
        scores = jnp.dot(block_queries, block_keys.T, preferred_element_type=jnp.float32)
        spread = cumulative[:, None, :] - cumulative[None, :, :]
        decays = jnp.where(causal_mask, jnp.exp(jnp.where(causal_mask, spread, 0.0)), 0.0)
        weights = (decays * scores[:, :, None] * block_steps[None, :, :]).astype(jnp.bfloat16)
        intra_out = jnp.einsum('qkh,khp->qhp', weights.astype(jnp.float32), block_vals.astype(jnp.float32), precision=highest)
        carried = jnp.exp(cumulative)[:, :, None] * jnp.einsum('qn,hnp->qhp', block_queries.astype(jnp.float32), carry_now, precision=highest)
        to_end = jnp.exp(cumulative[-1:, :] - cumulative) * block_steps
        factor = (to_end[:, :, None] * block_keys.astype(jnp.float32)[:, None, :]).astype(jnp.bfloat16)
        fresh_state = jnp.einsum('qhn,qhp->hnp', factor.astype(jnp.float32), block_vals.astype(jnp.float32), precision=highest)
        next_state = jnp.exp(cumulative[-1])[:, None, None] * carry_now + fresh_state
        output = intra_out + carried + skip_term[None, :, None] * block_vals.astype(jnp.float32)
        return (next_state, output)
    final_state, outputs = lax.scan(one_block, start_state.astype(jnp.float32), (values, keys_in, queries, rate_blocks, step_blocks))
    outputs = outputs.reshape(tokens, HEAD_COUNT, HEAD_DIM)
    mean_sq = lax.optimization_barrier(jnp.mean(outputs * outputs, axis=2, keepdims=True))
    normed = (outputs * lax.rsqrt(mean_sq + 1e-05)).reshape(tokens, channels)
    return (current.astype(jnp.float32) + gain_row.astype(jnp.float32) * normed).astype(jnp.bfloat16)

def reference(section_in, proj_weight, conv_weight, log_decay, step_size, skip_gain, norm_gain, carry_state, carry_rows):
    results = []
    for layer_id in range(SECTION_COUNT):
        produced = mamba_layer(section_in[layer_id], proj_weight[layer_id], conv_weight[layer_id], log_decay[layer_id], step_size[layer_id], skip_gain[layer_id], norm_gain[layer_id], carry_state[layer_id], carry_rows[layer_id])
        results.append(produced)
    handed = [results[SECTION_COUNT - 1]] + results[:SECTION_COUNT - 1]
    return jnp.stack(handed)
```

```python
import functools

import jax
import jax.numpy as jnp
from jax import lax
from jax.experimental import pallas as pl
from jax.experimental.pallas import tpu as pltpu
from jax.sharding import Mesh
from jax.sharding import PartitionSpec as P

HEADS = 64
DIM = 64
STATE = 128
TOK = 256
CH = 4096
LANES = 512
GROUPS = 8
ROWS = 16
LOG2E = 1.4426950408889634
CTX = ("x", "z", "core")
F32 = jnp.float32
BF16 = jnp.bfloat16
PARAMS = pltpu.CompilerParams(vmem_limit_bytes=56 * 2**20)


def dot(a, b):
    return jnp.dot(a, b, preferred_element_type=F32)


def parts(x, count):
    out = []
    for _ in range(count):
        piece = x.astype(BF16)
        out.append(piece)
        x = x - piece.astype(F32)
    return out


def iota(shape, axis):
    return lax.broadcasted_iota(jnp.int32, shape, axis)


def spread_matrix(rows, group, width):
    head = iota((rows, width), 1) // DIM + group * (LANES // DIM)
    return (iota((rows, width), 0) % HEADS == head).astype(F32).astype(BF16)


def conv_silu(pad, x, halo, taps):
    pad[0:16, :] = halo.astype(F32)
    pad[16:272, :] = x.astype(F32)
    total = taps[0:1] * pad[13:269, :]
    for j in range(1, 4):
        total = total + taps[j : j + 1] * pad[13 + j : 269 + j, :]
    return (total / (1.0 + jnp.exp(-total))).astype(BF16)


def first_kernel(
    first, u, halo, weight, taps, rates, steps, carried_bc, vals, bc, log_col, log_row, decay, pay, pad, lhs
):
    w = weight[...]
    projected = dot(u[...], w).astype(BF16)
    halo_bc = dot(halo[...], w).astype(BF16).astype(F32)
    halo_bc = jnp.where(first[0] == 1, carried_bc[...].astype(F32), halo_bc)
    for i in range(2):
        cols = slice(i * 128, (i + 1) * 128)
        bc[:, cols] = conv_silu(
            pad.at[i],
            projected[:, cols],
            halo_bc[:, cols],
            taps[:, CH + i * 128 : CH + (i + 1) * 128].astype(F32),
        )
    lhs[...] = bc[:, 0:128].astype(F32).T.astype(BF16)
    tri = (iota((TOK, TOK), 0) >= iota((TOK, TOK), 1)).astype(F32).astype(BF16)
    cum = sum(dot(tri, piece) for piece in parts(rates[...], 3))
    step = steps[...]
    last = cum[TOK - 1 : TOK]
    log2cum = cum * LOG2E
    log_col[...] = jnp.concatenate([log2cum, jnp.zeros_like(cum)], axis=1)
    row = log2cum - jnp.log2(step)
    log_row[...] = jnp.concatenate([row, row], axis=1).T[0:HEADS]
    to_end = jnp.concatenate(parts(jnp.exp(last - cum) * step, 2), axis=1)
    decay[...] = jnp.concatenate(parts(jnp.exp(cum), 2), axis=1)
    hi, mid, lo = parts(jnp.exp(last), 3)
    kind = iota((ROWS, HEADS), 0) // 4
    end_decay = jnp.where(
        kind == 0,
        hi.astype(F32),
        jnp.where(kind == 1, mid.astype(F32), jnp.where(kind == 2, lo.astype(F32), 0.0)),
    ).astype(BF16)
    row4 = iota((ROWS, 128), 0) % 4

    def one(q, _):
        base = pl.multiple_of(q * LANES, LANES)
        scale = dot(to_end, spread_matrix(2 * HEADS, q, LANES))
        ends = dot(end_decay, spread_matrix(HEADS, q, LANES))
        scaled = []
        for i in range(4):
            cols = pl.ds(pl.multiple_of(base + i * 128, 128), 128)
            act = conv_silu(pad.at[i], u[:, cols], halo[:, cols], taps[:, cols].astype(F32))
            vals[:, cols] = act
            scaled.append((act.astype(F32) * scale[:, i * 128 : (i + 1) * 128]).astype(BF16))
        fresh = dot(lhs[...], jnp.concatenate(scaled, axis=1)).astype(BF16)
        tail = jnp.zeros((ROWS, 128), F32)
        for i in range(4):
            tail = jnp.where(row4 == i, ends[:, i * 128 : (i + 1) * 128], tail)
        tail = tail.astype(BF16)
        core, x = q // 4, q % 4
        for g in range(8):
            owner = (x * 8 + g) * 2 + core
            pay[owner, :, 0:LANES] = fresh[g * ROWS : (g + 1) * ROWS]
            pay[owner, :, LANES : LANES + 128] = tail
        return 0

    lax.fori_loop(0, GROUPS, one, 0)


def scan_kernel(blocks, got, start, out):
    def one(i, state):
        out[i] = state.astype(BF16)
        tail = got[i, :, LANES : LANES + 128].astype(F32)
        tail = tail[0:4] + tail[4:8] + tail[8:12]
        ends = jnp.concatenate([tail[i : i + 1] for i in range(4)], axis=1)
        return state * ends + got[i, :, 0:LANES].astype(F32)

    lax.fori_loop(0, blocks, one, start[...])


def last_kernel(u, vals, bc, log_col, log_row, decay, starts, skip, gain, out, scores):
    q = pl.program_id(0)

    @pl.when(q == 0)
    def _():
        scores[...] = lax.dot_general(
            bc[:, 128:256], bc[:, 0:128], (((1,), (1,)), ((), ())), preferred_element_type=F32
        )

    core, x = q // 4, q % 4
    state = jnp.concatenate([starts[(x * 8 + g) * 2 + core] for g in range(8)], axis=0)
    carried = dot(bc[:, 128:256], state) * dot(decay[...], spread_matrix(2 * HEADS, q, LANES))
    cols = pltpu.roll(log_col[...], (128 - 8 * q) % 128, 1)
    rows = log_row[pl.ds(pl.multiple_of(q * 8, 8), 8), :]
    half = TOK // 2
    causal = iota((half, half), 0) >= iota((half, half), 1)
    left = iota((TOK, 128), 1) < DIM
    same = (iota((128, 128), 0) // DIM == iota((128, 128), 1) // DIM).astype(F32).astype(BF16)
    for i in range(4):
        lane = slice(i * 128, (i + 1) * 128)
        value = vals[:, lane]
        both = []
        for h in (2 * i, 2 * i + 1):
            col = cols[:, h : h + 1]
            row = rows[h : h + 1]
            top = jnp.exp2(jnp.where(causal, col[:half] - row[:, :half], -jnp.inf)) * scores[:half, :half]
            low_left = jnp.exp2(col[half:] - row[:, :half]) * scores[half:, :half]
            low_right = jnp.exp2(jnp.where(causal, col[half:] - row[:, half:], -jnp.inf)) * scores[half:, half:]
            low = jnp.concatenate([low_left.astype(BF16), low_right.astype(BF16)], axis=1)
            both.append(
                jnp.concatenate([dot(top.astype(BF16), value[:half]), dot(low, value)], axis=0)
            )
        result = jnp.where(left, both[0], both[1]) + carried[:, lane] + skip[:, lane] * value.astype(F32)
        mean_sq = dot((result * result).astype(BF16), same) * (1.0 / DIM)
        normed = result * lax.rsqrt(mean_sq + 1e-05)
        out[:, lane] = (u[:, lane].astype(F32) + gain[:, lane].astype(F32) * normed).astype(BF16)


def whole(*shape):
    return pl.BlockSpec(shape, lambda q: (0,) * len(shape))


def per_device(
    section_in, proj_weight, conv_weight, log_decay, step_size, skip_gain, norm_gain, carry_state, carry_rows
):
    u = section_in[0]
    place = lax.axis_index(CTX)
    first = place == 0
    behind = lax.ppermute(u[TOK - 16 :], CTX, [(i, i + 1) for i in range(63)])
    before = jnp.concatenate([jnp.zeros((13, CH + 256), BF16), carry_rows[0]], axis=0)
    halo = jnp.where(first, before[:, :CH], behind)
    vmem = pl.BlockSpec(memory_space=pltpu.VMEM)
    vals, bc, log_col, log_row, decay, pay = pl.pallas_call(
        first_kernel,
        out_shape=(
            jax.ShapeDtypeStruct((TOK, CH), BF16),
            jax.ShapeDtypeStruct((TOK, 256), BF16),
            jax.ShapeDtypeStruct((TOK, 128), F32),
            jax.ShapeDtypeStruct((HEADS, TOK), F32),
            jax.ShapeDtypeStruct((TOK, 128), BF16),
            jax.ShapeDtypeStruct((64, ROWS, LANES + 128), BF16),
        ),
        in_specs=[pl.BlockSpec(memory_space=pltpu.SMEM)] + [vmem] * 7,
        out_specs=[vmem] * 6,
        scratch_shapes=[pltpu.VMEM((4, 272, 128), F32), pltpu.VMEM((128, TOK), BF16)],
        compiler_params=PARAMS,
        name="first",
    )(
        first.astype(jnp.int32)[None],
        u,
        halo,
        proj_weight[0],
        conv_weight[0],
        log_decay[0],
        step_size[0],
        before[:, CH:],
    )
    got = lax.all_to_all(pay, CTX, 0, 0)
    head = (lax.axis_index("core") * 4 + lax.axis_index("x")) * 8
    start = lax.dynamic_slice(carry_state[0], (head, lax.axis_index("z") * ROWS, 0), (8, ROWS, DIM))
    start = start.transpose(1, 0, 2).reshape(ROWS, LANES)
    back = pl.pallas_call(
        functools.partial(scan_kernel, 64),
        out_shape=jax.ShapeDtypeStruct((64, ROWS, LANES), BF16),
        in_specs=[vmem] * 2,
        out_specs=vmem,
        compiler_params=PARAMS,
        name="scan",
    )(got, start)
    starts = lax.all_to_all(back, CTX, 0, 0)
    wide = pl.BlockSpec((TOK, LANES), lambda q: (0, q))
    line = pl.BlockSpec((1, LANES), lambda q: (0, q))
    rows = pl.pallas_call(
        last_kernel,
        grid=(GROUPS,),
        out_shape=jax.ShapeDtypeStruct((TOK, CH), BF16),
        in_specs=[
            wide,
            wide,
            whole(TOK, 256),
            whole(TOK, 128),
            whole(HEADS, TOK),
            whole(TOK, 128),
            whole(64, ROWS, LANES),
            line,
            line,
        ],
        out_specs=wide,
        scratch_shapes=[pltpu.VMEM((TOK, TOK), F32)],
        compiler_params=PARAMS,
        name="last",
    )(u, vals, bc, log_col, log_row, decay, starts, jnp.repeat(skip_gain, DIM, axis=1), norm_gain)
    handed = lax.ppermute(rows, "section", [(i, (i + 1) % 4) for i in range(4)])
    return handed[None]


def solution(mesh):
    split = Mesh(mesh.devices.reshape(4, 4, 8, 2), ("section",) + CTX)
    tokens = P("section", CTX, None)
    layer = P("section", None, None)
    return jax.shard_map(
        per_device,
        mesh=split,
        in_specs=(
            tokens,
            layer,
            layer,
            tokens,
            tokens,
            P("section", None),
            P("section", None),
            P("section", None, None, None),
            layer,
        ),
        out_specs=tokens,
        check_vma=False,
    )
```

```python
import functools

import jax
import jax.numpy as jnp
from jax import lax
from jax.experimental import pallas as pl
from jax.experimental.pallas import tpu as pltpu
from jax.sharding import Mesh
from jax.sharding import PartitionSpec as P

HEADS = 64
DIM = 64
STATE = 128
TOK = 256
CH = 4096
HALF = CH // 2
LANES = 512
GROUPS = 8
ROWS = 16
CHIPS = 32
LOG2E = 1.4426950408889634
F32 = jnp.float32
BF16 = jnp.bfloat16


def params(mib):
    return pltpu.CompilerParams(vmem_limit_bytes=mib * 2**20)


def cost(flops, moved, exps=0):
    return pl.CostEstimate(flops=int(flops), bytes_accessed=int(moved), transcendentals=int(exps))


def dot(a, b):
    return jnp.dot(a, b, preferred_element_type=F32)


def parts(x, count):
    out = []
    for _ in range(count):
        piece = x.astype(BF16)
        out.append(piece)
        x = x - piece.astype(F32)
    return out


def iota(shape, axis):
    return lax.broadcasted_iota(jnp.int32, shape, axis)


def two_parts(x):
    hi = x.astype(BF16).astype(F32)
    return jnp.where(iota(x.shape, 1) < HEADS, hi, x - hi).astype(BF16)


def spread_matrix(rows, group):
    head = iota((rows, LANES), 1) // DIM + group * (LANES // DIM)
    return (iota((rows, LANES), 0) % HEADS == head).astype(F32).astype(BF16)


def conv_silu(pad, x, halo, taps):
    pad[0:16, :] = halo.astype(F32)
    pad[16:272, :] = x.astype(F32)
    total = taps[0:1] * pad[13:269, :]
    for j in range(1, 4):
        total = total + taps[j : j + 1] * pad[13 + j : 269 + j, :]
    return (total / (1.0 + jnp.exp(-total))).astype(BF16)


def cumulated(rates):
    tri = (iota((TOK, TOK), 0) <= iota((TOK, TOK), 1)).astype(F32).astype(BF16)
    return sum(dot(piece, tri) for piece in parts(rates, 3))


def twice_turned(x):
    return jnp.concatenate([x, x], axis=0).T


def project_kernel(u, weight, rates, steps, projected, to_end, ends):
    projected[...] = dot(u[...], weight[...]).astype(BF16)
    cum = twice_turned(cumulated(rates[...]))
    last = cum[TOK - 1 : TOK]
    to_end[...] = two_parts(jnp.exp(last - cum) * twice_turned(steps[...]))
    hi, mid, lo = (piece.astype(F32) for piece in parts(jnp.exp(last), 3))
    kind = iota((ROWS, 128), 0) // 4
    tile = jnp.where(kind == 0, hi, jnp.where(kind == 1, mid, jnp.where(kind == 2, lo, 0.0)))
    ends[...] = jnp.where(iota((ROWS, 128), 1) < HEADS, tile, 0.0).astype(BF16)


def fresh_part(q, u, halo, taps, to_end, ends, turned, fresh, pad):
    spread = spread_matrix(2 * HEADS, q)
    scale = dot(to_end[...], spread)
    scaled = []
    for i in range(4):
        lane = slice(i * 128, (i + 1) * 128)
        act = conv_silu(pad.at[i], u[:, lane], halo[:, lane], taps[:, lane].astype(F32))
        scaled.append((act.astype(F32) * scale[:, lane]).astype(BF16))
    fresh[0:STATE, :] = dot(turned[...], jnp.concatenate(scaled, axis=1)).astype(BF16)
    fresh[STATE : STATE + ROWS, :] = dot(ends[...], spread).astype(BF16)


def send_kernel(
    flags, u, halo, taps, to_end, ends, all_halo, weight, projected, all_taps, carried_bc, par, fresh, turned, pack, pad
):
    step = pl.program_id(0)

    @pl.when(step == 0)
    def _():
        near = dot(all_halo[...], weight[...]).astype(BF16).astype(F32)
        near = jnp.where(flags[0] == 1, carried_bc[...].astype(F32), near)
        acts = []
        for i in range(2):
            lane = slice(i * 128, (i + 1) * 128)
            tap = all_taps[:, CH + i * 128 : CH + (i + 1) * 128].astype(F32)
            acts.append(conv_silu(pad.at[i], projected[:, lane], near[:, lane], tap))
        turned[...] = acts[0].astype(F32).T.astype(BF16)
        for s in range(16):
            for i in range(2):
                pack[s, :, i * 128 : (i + 1) * 128] = acts[i][s * 16 : (s + 1) * 16]
            lane = slice(s * 256, (s + 1) * 256)
            slab = jnp.where(
                iota((16, 256), 0) >= 13, all_halo[:, lane].astype(F32), par[:, lane].astype(F32)
            )
            pack[16 + s] = slab.astype(BF16)

    fresh_part(flags[1] * 4 + step, u, halo, taps, to_end, ends, turned, fresh, pad)


def keep_kernel(flags, u, halo, taps, to_end, ends, turned, fresh, pad):
    fresh_part(flags[2] * 4 + pl.program_id(0), u, halo, taps, to_end, ends, turned, fresh, pad)


def end_row(tail):
    tail = tail.astype(F32)
    return tail[0:1] + tail[4:5] + tail[8:9]


def join_kernel(flags, keep, got, pay, head_fresh):
    own, other = keep[0:STATE].astype(F32), got[0:STATE].astype(F32)
    own_end, other_end = end_row(keep[STATE:]), end_row(got[STATE:])
    lead = flags[2] == 0
    total = jnp.where(lead, other_end * own + other, own_end * other + own).astype(BF16)
    head_fresh[...] = jnp.where(lead, keep[...].astype(F32), got[...].astype(F32)).astype(BF16)
    pieces = [piece.astype(F32) for piece in parts(own_end * other_end, 3)]
    row = iota((ROWS, 128), 0)
    tail = jnp.zeros((ROWS, 128), F32)
    for p in range(3):
        for i in range(4):
            tail = jnp.where(row == 4 * p + i, pieces[p][:, i * 128 : (i + 1) * 128], tail)
    for g in range(8):
        pay[g, :, 0:LANES] = total[g * ROWS : (g + 1) * ROWS]
        pay[g, :, LANES : LANES + 128] = tail.astype(BF16)


def scan_kernel(got, start, out):
    def one(i, state):
        out[i] = state.astype(BF16)
        tail = got[i, :, LANES : LANES + 128].astype(F32)
        tail = tail[0:4] + tail[4:8] + tail[8:12]
        ends = jnp.concatenate([tail[i : i + 1] for i in range(4)], axis=1)
        return state * ends + got[i, :, 0:LANES].astype(F32)

    lax.fori_loop(0, CHIPS, one, start[...])


def start_kernel(flags, chip, head_fresh, mine, cross):
    state = jnp.concatenate([chip[g] for g in range(8)], axis=0).astype(F32)
    second = end_row(head_fresh[STATE:]) * state + head_fresh[0:STATE].astype(F32)
    lead = flags[2] == 0
    mine[...] = jnp.where(lead, state, second).astype(BF16)
    cross[...] = jnp.where(lead, second, state).astype(BF16)


def inner_kernel(u, pack, logs, partial, decay, scores, log_col, log_row, pad):
    q = pl.program_id(0)

    @pl.when(q == 0)
    def _():
        bc = pack[0:16].reshape(TOK, 256)
        scores[...] = lax.dot_general(
            bc[:, 128:256], bc[:, 0:128], (((1,), (1,)), ((), ())), preferred_element_type=F32
        )
        cum = cumulated(logs[0:HEADS])
        log_row[...] = cum * LOG2E - jnp.log2(logs[HEADS : 2 * HEADS])
        turned = twice_turned(cum)
        log_col[...] = turned * LOG2E
        decay[...] = two_parts(jnp.exp(turned))

    slab = jnp.concatenate([pack[16 + 2 * q], pack[17 + 2 * q]], axis=1).astype(F32)
    skip = slab[5:6] + slab[6:7] + slab[7:8]
    cols = pltpu.roll(log_col[...], (128 - 8 * q) % 128, 1)
    rows = log_row[pl.ds(pl.multiple_of(q * 8, 8), 8), :]
    half = TOK // 2
    causal = iota((half, half), 0) >= iota((half, half), 1)
    left = iota((TOK, 128), 1) < DIM
    for i in range(4):
        lane = slice(i * 128, (i + 1) * 128)
        value = conv_silu(pad.at[i], u[:, lane], slab[:, lane], slab[0:4, lane])
        both = []
        for h in (2 * i, 2 * i + 1):
            col = cols[:, h : h + 1]
            row = rows[h : h + 1]
            top = jnp.exp2(jnp.where(causal, col[:half] - row[:, :half], -jnp.inf)) * scores[:half, :half]
            low_left = jnp.exp2(col[half:] - row[:, :half]) * scores[half:, :half]
            low_right = jnp.exp2(jnp.where(causal, col[half:] - row[:, half:], -jnp.inf)) * scores[half:, half:]
            low = jnp.concatenate([low_left.astype(BF16), low_right.astype(BF16)], axis=1)
            both.append(jnp.concatenate([dot(top.astype(BF16), value[:half]), dot(low, value)], axis=0))
        partial[:, lane] = jnp.where(left, both[0], both[1]) + skip[:, lane] * value.astype(F32)


def outer_part(q, u, partial, starts, pack, decay, out):
    queries = pack[0:16].reshape(TOK, 256)[:, 128:256]
    carried = dot(queries, starts[...]) * dot(decay[...], spread_matrix(2 * HEADS, q))
    gain = jnp.concatenate([pack[16 + 2 * q], pack[17 + 2 * q]], axis=1).astype(F32)[4:5]
    same = (iota((128, 128), 0) // DIM == iota((128, 128), 1) // DIM).astype(F32).astype(BF16)
    for i in range(4):
        lane = slice(i * 128, (i + 1) * 128)
        result = partial[:, lane] + carried[:, lane]
        mean_sq = dot((result * result).astype(BF16), same) * (1.0 / DIM)
        normed = result * lax.rsqrt(mean_sq + 1e-05)
        out[:, lane] = (u[:, lane].astype(F32) + gain[:, lane] * normed).astype(BF16)


def outer_mine_kernel(flags, u, partial, starts, pack, decay, out):
    outer_part(flags[2] * 4 + pl.program_id(0), u, partial, starts, pack, decay, out)


def outer_other_kernel(flags, u, partial, starts, pack, decay, done, out):
    outer_part(flags[1] * 4 + pl.program_id(0), u, partial, starts, pack, decay, out)


def array(shape, dtype=BF16):
    return jax.ShapeDtypeStruct(shape, dtype)


def whole(*shape):
    return pl.BlockSpec(shape, lambda *_: (0,) * len(shape))


def half_columns(rows, which):
    return pl.BlockSpec((rows, LANES), lambda i, flags: (0, flags[which] * 4 + i))


def columns(rows):
    return pl.BlockSpec((rows, LANES), lambda i, *_: (0, i))


def call(kernel, name, out, grid, ins, outs, scratch=(), mib=16, prefetch=1, estimate=None, alias=None):
    return pl.pallas_call(
        kernel,
        out_shape=out,
        grid_spec=pltpu.PrefetchScalarGridSpec(
            num_scalar_prefetch=prefetch, grid=grid, in_specs=ins, out_specs=outs, scratch_shapes=list(scratch)
        ),
        compiler_params=params(mib),
        cost_estimate=estimate,
        input_output_aliases=alias or {},
        name=name,
    )


def exact(x):
    return lax.reduce_precision(x, 8, 7)


def per_device(
    section_in, proj_weight, conv_weight, log_decay, step_size, skip_gain, norm_gain, carry_state, carry_rows
):
    u = section_in[0]
    ctx = ("x", "z", "core")
    core = lax.axis_index("core")
    first = lax.axis_index(ctx) == 0
    flags = jnp.stack([first.astype(jnp.int32), 1 - core, core])

    def onward(value):
        return lax.ppermute(value, "section", [(i, (i + 1) % 4) for i in range(4)])

    def swapped(value):
        return lax.ppermute(value, "core", [(0, 1), (1, 0)])

    behind = lax.ppermute(u[TOK - 16 :], ctx, [(i, i + 1) for i in range(63)])
    next_u = onward(u)
    rates, steps = log_decay[0].T, step_size[0].T
    next_logs = onward(jnp.concatenate([rates, steps], axis=0))
    before = jnp.concatenate([jnp.zeros((13, CH + 256), BF16), carry_rows[0]], axis=0)
    halo = jnp.where(first, before[:, :CH], behind)
    skip = jnp.repeat(skip_gain, DIM, axis=1)
    skip_hi = exact(skip)
    skip_mid = exact(skip - skip_hi)
    skip_lo = skip - skip_hi - skip_mid
    par = jnp.concatenate(
        [conv_weight[0, :, :CH], norm_gain]
        + [piece.astype(BF16) for piece in (skip_hi, skip_mid, skip_lo)]
        + [jnp.zeros((8, CH), BF16)],
        axis=0,
    )
    vmem = pl.BlockSpec(memory_space=pltpu.VMEM)
    projected, to_end, ends = pl.pallas_call(
        project_kernel,
        out_shape=(array((TOK, 256)), array((TOK, 128)), array((ROWS, 128))),
        in_specs=[vmem] * 4,
        out_specs=[vmem] * 3,
        compiler_params=params(16),
        cost_estimate=cost(6e8, 4.5e6),
        name="project",
    )(u, proj_weight[0], rates, steps)

    pad = pltpu.VMEM((4, 272, 128), F32)
    ends_pad = whole(ROWS, 128)
    fresh_out = array((STATE + ROWS, HALF))
    send, turned, pack = call(
        send_kernel,
        "send",
        (fresh_out, array((STATE, TOK)), array((32, 16, 256))),
        (4,),
        [half_columns(TOK, 1), half_columns(16, 1), half_columns(4, 1), whole(TOK, 128), ends_pad]
        + [whole(16, CH), whole(CH, 256), whole(TOK, 256), whole(4, CH + 256), whole(16, 256), whole(16, CH)],
        [columns(STATE + ROWS), whole(STATE, TOK), whole(32, 16, 256)],
        [pad],
        mib=20,
        estimate=cost(6e8, 4.5e6, 5e5),
    )(
        flags, u, halo, conv_weight[0], to_end, ends, halo, proj_weight[0], projected, conv_weight[0],
        before[:, CH:], par,
    )
    got = swapped(send)
    keep = call(
        keep_kernel,
        "keep",
        fresh_out,
        (4,),
        [half_columns(TOK, 2), half_columns(16, 2), half_columns(4, 2), whole(TOK, 128), ends_pad, whole(STATE, TOK)],
        columns(STATE + ROWS),
        [pad],
        estimate=cost(6e8, 4.5e6, 5e5),
    )(flags, u, halo, conv_weight[0], to_end, ends, turned)
    pay, head_fresh = call(
        join_kernel,
        "join",
        (array((CHIPS, ROWS, LANES + 128)), fresh_out),
        (4,),
        [columns(STATE + ROWS)] * 2,
        [pl.BlockSpec((8, ROWS, LANES + 128), lambda i, *_: (i, 0, 0)), columns(STATE + ROWS)],
        estimate=cost(1e6, 2.5e6),
    )(flags, keep, got)
    shares = lax.all_to_all(pay, ("x", "z"), 0, 0)
    next_pack = onward(pack)
    next_fresh = onward(head_fresh)
    head = (core * 4 + lax.axis_index("x")) * 8
    start = lax.dynamic_slice(carry_state[0], (head, lax.axis_index("z") * ROWS, 0), (8, ROWS, DIM))
    start = start.transpose(1, 0, 2).reshape(ROWS, LANES)
    back = pl.pallas_call(
        scan_kernel,
        out_shape=array((CHIPS, ROWS, LANES)),
        in_specs=[vmem] * 2,
        out_specs=vmem,
        compiler_params=params(8),
        name="scan",
    )(shares, start)
    chip = lax.all_to_all(back, ("x", "z"), 0, 0)
    partial, decay = call(
        inner_kernel,
        "inner",
        (array((TOK, CH), F32), array((TOK, 128))),
        (GROUPS,),
        [columns(TOK), whole(32, 16, 256), whole(128, TOK)],
        [columns(TOK), whole(TOK, 128)],
        [pltpu.VMEM((TOK, TOK), F32), pltpu.VMEM((TOK, 128), F32), pltpu.VMEM((HEADS, TOK), F32), pad],
        mib=20,
        prefetch=0,
        estimate=cost(6e9, 9e6, 4e6),
    )(next_u, next_pack, next_logs)
    next_chip = onward(chip)
    state_half = array((STATE, HALF))
    mine, cross = call(
        start_kernel,
        "start",
        (state_half, state_half),
        (4,),
        [pl.BlockSpec((8, ROWS, LANES), lambda i, *_: (i, 0, 0)), columns(STATE + ROWS)],
        [columns(STATE)] * 2,
    )(flags, next_chip, next_fresh)
    other = swapped(cross)
    outer_in = [columns(STATE), whole(32, 16, 256), whole(TOK, 128)]
    rows = call(
        outer_mine_kernel,
        "outer_mine",
        array((TOK, CH)),
        (4,),
        [half_columns(TOK, 2), half_columns(TOK, 2)] + outer_in,
        half_columns(TOK, 2),
        estimate=cost(6e8, 5e6),
    )(flags, next_u, partial, mine, next_pack, decay)
    rows = call(
        outer_other_kernel,
        "outer_other",
        array((TOK, CH)),
        (4,),
        [half_columns(TOK, 1), half_columns(TOK, 1)] + outer_in + [pl.BlockSpec(memory_space=pl.ANY)],
        half_columns(TOK, 1),
        estimate=cost(6e8, 5e6),
        alias={6: 0},
    )(flags, next_u, partial, other, next_pack, decay, rows)
    return rows[None]


def solution(mesh):
    split = Mesh(mesh.devices.reshape(4, 4, 8, 2), ("section", "x", "z", "core"))
    tokens = P("section", ("x", "z", "core"), None)
    layer = P("section", None, None)
    return jax.shard_map(
        per_device,
        mesh=split,
        in_specs=(
            tokens,
            layer,
            layer,
            tokens,
            tokens,
            P("section", None),
            P("section", None),
            P("section", None, None, None),
            layer,
        ),
        out_specs=tokens,
        check_vma=False,
    )
```

```python
import functools

import jax
import jax.numpy as jnp
from jax import lax
from jax.experimental import pallas as pl
from jax.experimental.pallas import tpu as pltpu
from jax.sharding import Mesh
from jax.sharding import PartitionSpec as P

HEADS = 64
DIM = 64
STATE = 128
TOK = 256
CH = 4096
HALF = CH // 2
WIDE = 1024
LANES = 512
GROUPS = 8
ROWS = 16
CHIPS = 32
LOG2E = 1.4426950408889634
F32 = jnp.float32
BF16 = jnp.bfloat16


def params(mib):
    return pltpu.CompilerParams(vmem_limit_bytes=mib * 2**20)


def cost(flops, moved, exps=0):
    return pl.CostEstimate(flops=int(flops), bytes_accessed=int(moved), transcendentals=int(exps))


def dot(a, b):
    return jnp.dot(a, b, preferred_element_type=F32)


def parts(x, count):
    out = []
    for _ in range(count):
        piece = x.astype(BF16)
        out.append(piece)
        x = x - piece.astype(F32)
    return out


def iota(shape, axis):
    return lax.broadcasted_iota(jnp.int32, shape, axis)


def two_parts(x):
    hi = x.astype(BF16).astype(F32)
    return jnp.where(iota(x.shape, 1) < HEADS, hi, x - hi).astype(BF16)


def spread_matrix(rows, group):
    head = iota((rows, LANES), 1) // DIM + group * (LANES // DIM)
    return (iota((rows, LANES), 0) % HEADS == head).astype(F32).astype(BF16)


def conv_silu(pad, x, halo, taps):
    pad[0:16, :] = halo.astype(F32)
    pad[16:272, :] = x.astype(F32)
    total = taps[0:1] * pad[13:269, :]
    for j in range(1, 4):
        total = total + taps[j : j + 1] * pad[13 + j : 269 + j, :]
    half = 0.5 * total
    return (half + half * jnp.tanh(half)).astype(BF16)


def cumulated(rates):
    tri = (iota((TOK, TOK), 0) <= iota((TOK, TOK), 1)).astype(F32).astype(BF16)
    return sum(dot(piece, tri) for piece in parts(rates, 3))


def twice_turned(x):
    return jnp.concatenate([x, x], axis=0).T


def end_factors(cum, steps):
    last = cum[TOK - 1 : TOK]
    hi, mid, lo = (piece.astype(F32) for piece in parts(jnp.exp(last), 3))
    kind = iota((ROWS, 128), 0) // 4
    tile = jnp.where(kind == 0, hi, jnp.where(kind == 1, mid, jnp.where(kind == 2, lo, 0.0)))
    ends = jnp.where(iota((ROWS, 128), 1) < HEADS, tile, 0.0).astype(BF16)
    return two_parts(jnp.exp(last - cum) * steps), ends


def project_kernel(u, weight, rates, steps, projected, to_end, ends, edge, total):
    step = pl.program_id(0)

    @pl.when(step == 0)
    def _():
        total[...] = jnp.zeros_like(total)
        to_end[...], ends[...] = end_factors(twice_turned(cumulated(rates[...])), twice_turned(steps[...]))

    edge[:, pl.ds(pl.multiple_of(step * 1024, 1024), 1024)] = u[TOK - 16 : TOK]
    total[...] += dot(u[...], weight[...])

    @pl.when(step == 3)
    def _():
        rounded = total[...].astype(BF16)
        projected[...] = rounded
        edge[:, CH:] = rounded[TOK - 16 : TOK]


def fresh_part(q, first, u, behind, before, taps, to_end, ends, turned, fresh, pad):
    spread = spread_matrix(2 * HEADS, q)
    scale = dot(to_end[...], spread)
    halo = jnp.where(first == 1, before[...].astype(F32), behind[...].astype(F32))
    scaled = []
    for i in range(4):
        lane = slice(i * 128, (i + 1) * 128)
        act = conv_silu(pad.at[i], u[:, lane], halo[:, lane], taps[:, lane].astype(F32))
        scaled.append((act.astype(F32) * scale[:, lane]).astype(BF16))
    fresh[0:STATE, :] = dot(turned[...], jnp.concatenate(scaled, axis=1)).astype(BF16)
    fresh[STATE : STATE + ROWS, :] = dot(ends[...], spread).astype(BF16)


def send_kernel(
    flags, u, behind, before, taps, to_end, ends, all_behind, all_before, projected, all_taps, par, fresh, turned, pack, pad
):
    step = pl.program_id(0)

    @pl.when(step == 0)
    def _():
        near = jnp.where(flags[0] == 1, all_before[...].astype(F32), all_behind[...].astype(F32))
        acts = []
        for i in range(2):
            lane = slice(CH + i * 128, CH + (i + 1) * 128)
            value = projected[:, i * 128 : (i + 1) * 128]
            acts.append(conv_silu(pad.at[i], value, near[:, lane], all_taps[:, lane].astype(F32)))
        turned[...] = acts[0].astype(F32).T.astype(BF16)
        for s in range(16):
            for i in range(2):
                pack[s, :, i * 128 : (i + 1) * 128] = acts[i][s * 16 : (s + 1) * 16]
            lane = slice(s * 256, (s + 1) * 256)
            slab = jnp.where(iota((16, 256), 0) >= 13, near[:, lane], par[:, lane].astype(F32))
            pack[16 + s] = slab.astype(BF16)

    fresh_part(flags[1] * 4 + step, flags[0], u, behind, before, taps, to_end, ends, turned, fresh, pad)


def keep_kernel(flags, u, behind, before, taps, to_end, ends, turned, fresh, pad):
    q = flags[2] * 4 + pl.program_id(0)
    fresh_part(q, flags[0], u, behind, before, taps, to_end, ends, turned, fresh, pad)


def end_row(tail):
    tail = tail.astype(F32)
    return tail[0:1] + tail[4:5] + tail[8:9]


def join_kernel(flags, keep, got, pay):
    own, other = keep[0:STATE].astype(F32), got[0:STATE].astype(F32)
    own_end, other_end = end_row(keep[STATE:]), end_row(got[STATE:])
    lead = flags[2] == 0
    total = jnp.where(lead, other_end * own + other, own_end * other + own).astype(BF16)
    pieces = [piece.astype(F32) for piece in parts(own_end * other_end, 3)]
    row = iota((ROWS, 128), 0)
    tail = jnp.zeros((ROWS, 128), F32)
    for p in range(3):
        for i in range(4):
            tail = jnp.where(row == 4 * p + i, pieces[p][:, i * 128 : (i + 1) * 128], tail)
    for g in range(8):
        pay[g, :, 0:LANES] = total[g * ROWS : (g + 1) * ROWS]
        pay[g, :, LANES : LANES + 128] = tail.astype(BF16)


def scan_kernel(got, start, out):
    def one(i, state):
        out[i] = state.astype(BF16)
        tail = got[i, :, LANES : LANES + 128].astype(F32)
        tail = tail[0:4] + tail[4:8] + tail[8:12]
        ends = jnp.concatenate([tail[i : i + 1] for i in range(4)], axis=1)
        return state * ends + got[i, :, 0:LANES].astype(F32)

    lax.fori_loop(0, CHIPS, one, start[...])


def start_kernel(flags, chip, low_fresh, lead_fresh, mine, cross):
    state = jnp.concatenate([chip[g] for g in range(8)], axis=0).astype(F32)
    lead = flags[2] == 0
    fresh = jnp.where(lead, low_fresh[...].astype(F32), lead_fresh[...].astype(F32))
    second = end_row(fresh[STATE:]) * state + fresh[0:STATE]
    mine[...] = jnp.where(lead, state, second).astype(BF16)
    cross[...] = jnp.where(lead, second, state).astype(BF16)


def inner_kernel(
    u, pack, logs, partial, decay, low_fresh, high_fresh, scores, log_col, log_row, turned_keys, to_end, ends, pad
):
    q = pl.program_id(0)

    @pl.when(q == 0)
    def _():
        bc = pack[0:16].reshape(TOK, 256)
        scores[...] = lax.dot_general(
            bc[:, 128:256], bc[:, 0:128], (((1,), (1,)), ((), ())), preferred_element_type=F32
        )
        cum = cumulated(logs[0:HEADS])
        log_row[...] = cum * LOG2E - jnp.log2(logs[HEADS : 2 * HEADS])
        turned = twice_turned(cum)
        log_col[...] = turned * LOG2E
        decay[...] = two_parts(jnp.exp(turned))
        turned_keys[...] = bc[:, 0:128].astype(F32).T.astype(BF16)
        to_end[...], ends[...] = end_factors(turned, twice_turned(logs[HEADS : 2 * HEADS]))

    slab = jnp.concatenate([pack[16 + 2 * q], pack[17 + 2 * q]], axis=1).astype(F32)
    skip = slab[5:6] + slab[6:7] + slab[7:8]
    spread = spread_matrix(2 * HEADS, q)
    scale = dot(to_end[...], spread)
    scaled = []
    cols = pltpu.roll(log_col[...], (128 - 8 * q) % 128, 1)
    rows = log_row[pl.ds(pl.multiple_of(q * 8, 8), 8), :]
    half = TOK // 2
    causal = iota((half, half), 0) >= iota((half, half), 1)
    left = iota((TOK, 128), 1) < DIM
    for i in range(4):
        lane = slice(i * 128, (i + 1) * 128)
        value = conv_silu(pad.at[i], u[:, lane], slab[:, lane], slab[0:4, lane])
        scaled.append((value.astype(F32) * scale[:, lane]).astype(BF16))
        both = []
        for h in (2 * i, 2 * i + 1):
            col = cols[:, h : h + 1]
            row = rows[h : h + 1]
            top = jnp.exp2(jnp.where(causal, col[:half] - row[:, :half], -jnp.inf)) * scores[:half, :half]
            low_left = jnp.exp2(col[half:] - row[:, :half]) * scores[half:, :half]
            low_right = jnp.exp2(jnp.where(causal, col[half:] - row[:, half:], -jnp.inf)) * scores[half:, half:]
            low = jnp.concatenate([low_left.astype(BF16), low_right.astype(BF16)], axis=1)
            both.append(jnp.concatenate([dot(top.astype(BF16), value[:half]), dot(low, value)], axis=0))
        partial[:, lane] = jnp.where(left, both[0], both[1]) + skip[:, lane] * value.astype(F32)
    fresh = dot(turned_keys[...], jnp.concatenate(scaled, axis=1)).astype(BF16)
    end_rows = dot(ends[...], spread).astype(BF16)

    @pl.when(q < 4)
    def _():
        low_fresh[0:STATE, :] = fresh
        low_fresh[STATE:, :] = end_rows

    @pl.when(q >= 4)
    def _():
        high_fresh[0:STATE, :] = fresh
        high_fresh[STATE:, :] = end_rows


def mark_kernel(*refs):
    pass


def outer_part(half, u, partial, starts, pack, decay, out):
    step = pl.program_id(0)
    queries = pack[0:16].reshape(TOK, 256)[:, 128:256]
    head = iota((2 * HEADS, WIDE), 1) // DIM + (half * 2 + step) * (WIDE // DIM)
    spread = (iota((2 * HEADS, WIDE), 0) % HEADS == head).astype(F32).astype(BF16)
    carried = dot(queries, starts[...]) * dot(decay[...], spread)
    slabs = [pack[16 + half * 8 + step * 4 + i] for i in range(4)]
    gain = jnp.concatenate(slabs, axis=1).astype(F32)[4:5]
    same = (iota((128, 128), 0) // DIM == iota((128, 128), 1) // DIM).astype(F32).astype(BF16)
    for i in range(WIDE // 128):
        lane = slice(i * 128, (i + 1) * 128)
        result = partial[:, lane] + carried[:, lane]
        mean_sq = dot((result * result).astype(BF16), same) * (1.0 / DIM)
        normed = result * lax.rsqrt(mean_sq + 1e-05)
        out[:, lane] = (u[:, lane].astype(F32) + gain[:, lane] * normed).astype(BF16)


def outer_mine_kernel(flags, u, partial, starts, pack, decay, out):
    outer_part(flags[2], u, partial, starts, pack, decay, out)


def outer_other_kernel(flags, u, partial, starts, pack, decay, done, out):
    outer_part(flags[1], u, partial, starts, pack, decay, out)


def array(shape, dtype=BF16):
    return jax.ShapeDtypeStruct(shape, dtype)


def whole(*shape):
    return pl.BlockSpec(shape, lambda *_: (0,) * len(shape))


def half_columns(rows, which):
    return pl.BlockSpec((rows, LANES), lambda i, flags: (0, flags[which] * 4 + i))


def wide_columns(rows, which):
    return pl.BlockSpec((rows, WIDE), lambda i, flags: (0, flags[which] * 2 + i))


def columns(rows):
    return pl.BlockSpec((rows, LANES), lambda i, *_: (0, i))


def call(kernel, name, out, grid, ins, outs, scratch=(), mib=16, prefetch=1, estimate=None, alias=None):
    return pl.pallas_call(
        kernel,
        out_shape=out,
        grid_spec=pltpu.PrefetchScalarGridSpec(
            num_scalar_prefetch=prefetch, grid=grid, in_specs=ins, out_specs=outs, scratch_shapes=list(scratch)
        ),
        compiler_params=params(mib),
        cost_estimate=estimate,
        input_output_aliases=alias or {},
        name=name,
    )


def mark(value, *others):
    place = pl.BlockSpec(memory_space=pl.ANY)
    return pl.pallas_call(
        mark_kernel,
        out_shape=array(value.shape, value.dtype),
        in_specs=[place] * (1 + len(others)),
        out_specs=place,
        input_output_aliases={0: 0},
        cost_estimate=cost(6e9, 9e6, 4e6),
        compiler_params=params(2),
        name="mark",
    )(value, *others)


def exact(x):
    return lax.reduce_precision(x, 8, 7)


def per_device(
    section_in, proj_weight, conv_weight, log_decay, step_size, skip_gain, norm_gain, carry_state, carry_rows
):
    u = section_in[0]
    ctx = ("x", "z", "core")
    core = lax.axis_index("core")
    first = lax.axis_index(ctx) == 0
    flags = jnp.stack([first.astype(jnp.int32), 1 - core, core])

    def onward(value):
        return lax.ppermute(value, "section", [(i, (i + 1) % 4) for i in range(4)])

    def swapped(value):
        return lax.ppermute(value, "core", [(0, 1), (1, 0)])

    rates, steps = log_decay[0].T, step_size[0].T
    projected, to_end, ends, edge = pl.pallas_call(
        project_kernel,
        grid=(4,),
        out_shape=(
            array((TOK, 256)),
            array((TOK, 128)),
            array((ROWS, 128)),
            array((16, CH + 256)),
        ),
        in_specs=[
            pl.BlockSpec((TOK, 1024), lambda i: (0, i)),
            pl.BlockSpec((1024, 256), lambda i: (i, 0)),
            whole(HEADS, TOK),
            whole(HEADS, TOK),
        ],
        out_specs=[
            whole(TOK, 256),
            whole(TOK, 128),
            whole(ROWS, 128),
            whole(16, CH + 256),
        ],
        scratch_shapes=[pltpu.VMEM((TOK, 256), F32)],
        compiler_params=params(16),
        cost_estimate=cost(6e8, 4.5e6),
        name="project",
    )(u, proj_weight[0], rates, steps)
    behind = lax.ppermute(edge, ctx, [(i, i + 1) for i in range(63)])
    next_u = onward(u)
    next_logs = onward(jnp.concatenate([rates, steps], axis=0))
    before = jnp.concatenate([jnp.zeros((13, CH + 256), BF16), carry_rows[0]], axis=0)
    skip = jnp.repeat(skip_gain, DIM, axis=1)
    skip_hi = exact(skip)
    skip_mid = exact(skip - skip_hi)
    skip_lo = skip - skip_hi - skip_mid
    par = jnp.concatenate(
        [conv_weight[0, :, :CH], norm_gain]
        + [piece.astype(BF16) for piece in (skip_hi, skip_mid, skip_lo)]
        + [jnp.zeros((8, CH), BF16)],
        axis=0,
    )
    behind, before, par = lax.optimization_barrier((behind, before, par))
    vmem = pl.BlockSpec(memory_space=pltpu.VMEM)

    pad = pltpu.VMEM((4, 272, 128), F32)
    fresh_out = array((STATE + ROWS, HALF))

    def columns_of(which):
        return [half_columns(rows, which) for rows in (TOK, 16, 16, 4)] + [whole(TOK, 128), whole(ROWS, 128)]

    send, turned, pack = call(
        send_kernel,
        "send",
        (fresh_out, array((STATE, TOK)), array((32, 16, 256))),
        (4,),
        columns_of(1)
        + [whole(16, CH + 256), whole(16, CH + 256), whole(TOK, 256), whole(4, CH + 256), whole(16, CH)],
        [columns(STATE + ROWS), whole(STATE, TOK), whole(32, 16, 256)],
        [pad],
        mib=16,
        estimate=cost(6e8, 4.5e6, 5e5),
    )(
        flags, u, behind, before, conv_weight[0], to_end, ends, behind, before, projected, conv_weight[0], par
    )
    next_pack = onward(pack)
    got = swapped(send)
    keep = call(
        keep_kernel,
        "keep",
        fresh_out,
        (4,),
        columns_of(2) + [whole(STATE, TOK)],
        columns(STATE + ROWS),
        [pad],
        mib=16,
        estimate=cost(6e8, 4.5e6, 5e5),
    )(flags, u, behind, before, conv_weight[0], to_end, ends, turned)
    pay = call(
        join_kernel,
        "join",
        array((CHIPS, ROWS, LANES + 128)),
        (4,),
        [columns(STATE + ROWS)] * 2,
        pl.BlockSpec((8, ROWS, LANES + 128), lambda i, *_: (i, 0, 0)),
        estimate=cost(1e6, 2.5e6),
    )(flags, keep, got)
    shares = lax.all_to_all(pay, ("x", "z"), 0, 0)
    head = (core * 4 + lax.axis_index("x")) * 8
    start = lax.dynamic_slice(carry_state[0], (head, lax.axis_index("z") * ROWS, 0), (8, ROWS, DIM))
    start = start.transpose(1, 0, 2).reshape(ROWS, LANES)
    back = pl.pallas_call(
        scan_kernel,
        out_shape=array((CHIPS, ROWS, LANES)),
        in_specs=[vmem] * 2,
        out_specs=vmem,
        compiler_params=params(8),
        name="scan",
    )(shares, start)
    chip = lax.all_to_all(back, ("x", "z"), 0, 0)
    next_u = mark(next_u, next_pack, next_logs)
    chip, next_u, next_pack, next_logs = lax.optimization_barrier((chip, next_u, next_pack, next_logs))
    next_chip = onward(chip)
    next_chip = mark(next_chip)
    partial, decay, low_fresh, high_fresh = call(
        inner_kernel,
        "inner",
        (array((TOK, CH), F32), array((TOK, 128)), fresh_out, fresh_out),
        (GROUPS,),
        [columns(TOK), whole(32, 16, 256), whole(128, TOK)],
        [
            columns(TOK),
            whole(TOK, 128),
            pl.BlockSpec((STATE + ROWS, LANES), lambda q: (0, jnp.minimum(q, 3))),
            pl.BlockSpec((STATE + ROWS, LANES), lambda q: (0, jnp.maximum(q - 4, 0))),
        ],
        [
            pltpu.VMEM((TOK, TOK), F32),
            pltpu.VMEM((TOK, 128), F32),
            pltpu.VMEM((HEADS, TOK), F32),
            pltpu.VMEM((STATE, TOK), BF16),
            pltpu.VMEM((TOK, 128), BF16),
            pltpu.VMEM((ROWS, 128), BF16),
            pad,
        ],
        mib=20,
        prefetch=0,
        estimate=cost(1, 1),
    )(next_u, next_pack, next_logs)
    lead_fresh = lax.ppermute(high_fresh, "core", [(0, 1)])
    state_half = array((STATE, HALF))
    mine, cross = call(
        start_kernel,
        "start",
        (state_half, state_half),
        (4,),
        [pl.BlockSpec((8, ROWS, LANES), lambda i, *_: (i, 0, 0)), columns(STATE + ROWS), columns(STATE + ROWS)],
        [columns(STATE)] * 2,
    )(flags, next_chip, low_fresh, lead_fresh)
    other = swapped(cross)
    outer_in = [pl.BlockSpec((STATE, WIDE), lambda i, *_: (0, i)), whole(32, 16, 256), whole(TOK, 128)]
    rows = call(
        outer_mine_kernel,
        "outer_mine",
        array((TOK, CH)),
        (2,),
        [wide_columns(TOK, 2), wide_columns(TOK, 2)] + outer_in,
        wide_columns(TOK, 2),
        estimate=cost(6e8, 5e6),
    )(flags, next_u, partial, mine, next_pack, decay)
    rows = call(
        outer_other_kernel,
        "outer_other",
        array((TOK, CH)),
        (2,),
        [wide_columns(TOK, 1), wide_columns(TOK, 1)] + outer_in + [pl.BlockSpec(memory_space=pl.ANY)],
        wide_columns(TOK, 1),
        estimate=cost(6e8, 5e6),
        alias={6: 0},
    )(flags, next_u, partial, other, next_pack, decay, rows)
    return rows[None]


def solution(mesh):
    split = Mesh(mesh.devices.reshape(4, 4, 8, 2), ("section", "x", "z", "core"))
    tokens = P("section", ("x", "z", "core"), None)
    layer = P("section", None, None)
    return jax.shard_map(
        per_device,
        mesh=split,
        in_specs=(
            tokens,
            layer,
            layer,
            tokens,
            tokens,
            P("section", None),
            P("section", None),
            P("section", None, None, None),
            layer,
        ),
        out_specs=tokens,
        check_vma=False,
    )
```

```python
import functools

import jax
import jax.numpy as jnp
from jax import lax
from jax.experimental import pallas as pl
from jax.experimental.pallas import tpu as pltpu
from jax.sharding import Mesh
from jax.sharding import PartitionSpec as P

HEADS = 64
DIM = 64
STATE = 128
TOK = 256
CH = 4096
HALF = CH // 2
LANES = 512
GROUPS = 8
ROWS = 16
CHIPS = 32
LOG2E = 1.4426950408889634
F32 = jnp.float32
BF16 = jnp.bfloat16


def params(mib):
    return pltpu.CompilerParams(vmem_limit_bytes=mib * 2**20)


def cost(flops, moved, exps=0):
    return pl.CostEstimate(flops=int(flops), bytes_accessed=int(moved), transcendentals=int(exps))


def dot(a, b):
    return jnp.dot(a, b, preferred_element_type=F32)


def parts(x, count):
    out = []
    for _ in range(count):
        piece = x.astype(BF16)
        out.append(piece)
        x = x - piece.astype(F32)
    return out


def iota(shape, axis):
    return lax.broadcasted_iota(jnp.int32, shape, axis)


def two_parts(x):
    hi = x.astype(BF16).astype(F32)
    return jnp.where(iota(x.shape, 1) < HEADS, hi, x - hi).astype(BF16)


def spread_matrix(rows, group):
    head = iota((rows, LANES), 1) // DIM + group * (LANES // DIM)
    return (iota((rows, LANES), 0) % HEADS == head).astype(F32).astype(BF16)


def conv_silu(pad, x, halo, taps, first=None, carried=None):
    pad[0:16, :] = halo.astype(F32)
    if carried is not None:
        pad[13:16, :] = jnp.where(first == 1, carried.astype(F32), halo.astype(F32)[13:16])
    pad[16:272, :] = x.astype(F32)
    total = taps[0:1] * pad[13:269, :]
    for j in range(1, 4):
        total = total + taps[j : j + 1] * pad[13 + j : 269 + j, :]
    half = 0.5 * total
    return (half + half * jnp.tanh(half)).astype(BF16)


def cumulated(rates):
    tri = (iota((TOK, TOK), 0) <= iota((TOK, TOK), 1)).astype(F32).astype(BF16)
    return sum(dot(piece, tri) for piece in parts(rates, 3))


def twice_turned(x):
    return jnp.concatenate([x, x], axis=0).T


def end_factors(cum, steps):
    last = cum[TOK - 1 : TOK]
    hi, mid, lo = (piece.astype(F32) for piece in parts(jnp.exp(last), 3))
    kind = iota((ROWS, 128), 0) // 4
    tile = jnp.where(kind == 0, hi, jnp.where(kind == 1, mid, jnp.where(kind == 2, lo, 0.0)))
    ends = jnp.where(iota((ROWS, 128), 1) < HEADS, tile, 0.0).astype(BF16)
    return two_parts(jnp.exp(last - cum) * steps), ends


def fresh_half(half, first, u, behind, carried, taps, to_end, ends, turned, fresh, pad):
    for q in range(4):
        spread = spread_matrix(2 * HEADS, half * 4 + q)
        scale = dot(to_end[...], spread)
        scaled = []
        for i in range(4):
            lane = pl.ds(pl.multiple_of(half * HALF + q * LANES + i * 128, 128), 128)
            act = conv_silu(
                pad.at[i], u[:, lane], behind[:, lane], taps[:, lane].astype(F32), first, carried[:, lane]
            )
            scaled.append((act.astype(F32) * scale[:, i * 128 : (i + 1) * 128]).astype(BF16))
        cols = slice(q * LANES, (q + 1) * LANES)
        fresh[0:STATE, cols] = dot(turned[...], jnp.concatenate(scaled, axis=1)).astype(BF16)
        fresh[STATE : STATE + ROWS, cols] = dot(ends[...], spread).astype(BF16)


def fetch_kernel(u, weight, near_u, near_weight, sems):
    copies = []
    for i in range(4):
        rows, depth = pl.ds(i * 64, 64), pl.ds(i * 1024, 1024)
        copies.append(pltpu.make_async_copy(u.at[rows], near_u.at[rows], sems.at[2 * i]))
        copies.append(pltpu.make_async_copy(weight.at[depth], near_weight.at[depth], sems.at[2 * i + 1]))
    for copy in copies:
        copy.start()
    for copy in copies:
        copy.wait()


def send_kernel(
    flags, u, weight, logs, behind, carried, taps, fresh, turned, pack, to_end, ends, pad
):
    first = flags[0]
    to_end[...], ends[...] = end_factors(
        twice_turned(cumulated(logs[0:HEADS])), twice_turned(logs[HEADS : 2 * HEADS])
    )
    projected = dot(u[...], weight[...]).astype(BF16)
    rim_bc = dot(behind[...], weight[...]).astype(BF16).astype(F32)
    acts = []
    for i in range(2):
        lane = slice(CH + i * 128, CH + (i + 1) * 128)
        value, rim = projected[:, i * 128 : (i + 1) * 128], rim_bc[:, i * 128 : (i + 1) * 128]
        acts.append(conv_silu(pad.at[i], value, rim, taps[:, lane].astype(F32), first, carried[:, lane]))
    turned[...] = acts[0].astype(F32).T.astype(BF16)
    for s in range(16):
        for i in range(2):
            pack[s, :, i * 128 : (i + 1) * 128] = acts[i][s * 16 : (s + 1) * 16]
    fresh_half(flags[1], first, u, behind, carried, taps, to_end, ends, turned, fresh, pad)


def keep_kernel(flags, u, behind, carried, taps, to_end, ends, turned, fresh, pad):
    fresh_half(flags[2], flags[0], u, behind, carried, taps, to_end, ends, turned, fresh, pad)


def end_row(tail):
    tail = tail.astype(F32)
    return tail[0:1] + tail[4:5] + tail[8:9]


def join_kernel(flags, keep, got, pay):
    lead = flags[2] == 0
    row = iota((ROWS, 128), 0)
    for q in range(4):
        cols = slice(q * LANES, (q + 1) * LANES)
        own, other = keep[0:STATE, cols].astype(F32), got[0:STATE, cols].astype(F32)
        own_end, other_end = end_row(keep[STATE:, cols]), end_row(got[STATE:, cols])
        total = jnp.where(lead, other_end * own + other, own_end * other + own).astype(BF16)
        pieces = [piece.astype(F32) for piece in parts(own_end * other_end, 3)]
        tail = jnp.zeros((ROWS, 128), F32)
        for p in range(3):
            for i in range(4):
                tail = jnp.where(row == 4 * p + i, pieces[p][:, i * 128 : (i + 1) * 128], tail)
        tail = tail.astype(BF16)
        for g in range(8):
            pay[q * 8 + g, :, 0:LANES] = total[g * ROWS : (g + 1) * ROWS]
            pay[q * 8 + g, :, LANES : LANES + 128] = tail


def scan_kernel(got, start, out):
    def one(i, state):
        out[i] = state.astype(BF16)
        tail = got[i, :, LANES : LANES + 128].astype(F32)
        tail = tail[0:4] + tail[4:8] + tail[8:12]
        ends = jnp.concatenate([tail[i : i + 1] for i in range(4)], axis=1)
        return state * ends + got[i, :, 0:LANES].astype(F32)

    lax.fori_loop(0, CHIPS, one, start[...])


def start_kernel(flags, chip, low_fresh, lead_fresh, mine, cross):
    lead = flags[2] == 0
    for q in range(4):
        cols = slice(q * LANES, (q + 1) * LANES)
        state = jnp.concatenate([chip[q * 8 + g] for g in range(8)], axis=0).astype(F32)
        fresh = jnp.where(lead, low_fresh[:, cols].astype(F32), lead_fresh[:, cols].astype(F32))
        second = end_row(fresh[STATE:]) * state + fresh[0:STATE]
        mine[:, cols] = jnp.where(lead, state, second).astype(BF16)
        cross[:, cols] = jnp.where(lead, second, state).astype(BF16)


def inner_kernel(
    u, pack, par, logs, partial, decay, far_u, low_fresh, high_fresh, scores, log_col, log_row, turned_keys, to_end, ends, pad
):
    q = pl.program_id(0)

    @pl.when(q == 0)
    def _():
        bc = pack[...].reshape(TOK, 256)
        scores[...] = lax.dot_general(
            bc[:, 128:256], bc[:, 0:128], (((1,), (1,)), ((), ())), preferred_element_type=F32
        )
        cum = cumulated(logs[0:HEADS])
        log_row[...] = cum * LOG2E - jnp.log2(logs[HEADS : 2 * HEADS])
        turned = twice_turned(cum)
        log_col[...] = turned * LOG2E
        decay[...] = two_parts(jnp.exp(turned))
        turned_keys[...] = bc[:, 0:128].astype(F32).T.astype(BF16)
        to_end[...], ends[...] = end_factors(turned, twice_turned(logs[HEADS : 2 * HEADS]))

    far_u[...] = u[...]
    slab = par[...].astype(F32)
    skip = slab[5:6] + slab[6:7] + slab[7:8]
    spread = spread_matrix(2 * HEADS, q)
    scale = dot(to_end[...], spread)
    scaled = []
    cols = pltpu.roll(log_col[...], (128 - 8 * q) % 128, 1)
    rows = log_row[pl.ds(pl.multiple_of(q * 8, 8), 8), :]
    half = TOK // 2
    causal = iota((half, half), 0) >= iota((half, half), 1)
    left = iota((TOK, 128), 1) < DIM
    for i in range(4):
        lane = slice(i * 128, (i + 1) * 128)
        value = conv_silu(pad.at[i], u[:, lane], slab[:, lane], slab[0:4, lane])
        scaled.append((value.astype(F32) * scale[:, lane]).astype(BF16))
        both = []
        for h in (2 * i, 2 * i + 1):
            col = cols[:, h : h + 1]
            row = rows[h : h + 1]
            top = jnp.exp2(jnp.where(causal, col[:half] - row[:, :half], -jnp.inf)) * scores[:half, :half]
            low_left = jnp.exp2(col[half:] - row[:, :half]) * scores[half:, :half]
            low_right = jnp.exp2(jnp.where(causal, col[half:] - row[:, half:], -jnp.inf)) * scores[half:, half:]
            low = jnp.concatenate([low_left.astype(BF16), low_right.astype(BF16)], axis=1)
            both.append(jnp.concatenate([dot(top.astype(BF16), value[:half]), dot(low, value)], axis=0))
        partial[:, lane] = jnp.where(left, both[0], both[1]) + skip[:, lane] * value.astype(F32)
    fresh = dot(turned_keys[...], jnp.concatenate(scaled, axis=1)).astype(BF16)
    end_rows = dot(ends[...], spread).astype(BF16)

    @pl.when(q < 4)
    def _():
        low_fresh[0:STATE, :] = fresh
        low_fresh[STATE:, :] = end_rows

    @pl.when(q >= 4)
    def _():
        high_fresh[0:STATE, :] = fresh
        high_fresh[STATE:, :] = end_rows


def mark_kernel(*refs):
    pass


def outer_half(half, u, partial, starts, pack, par, decay, out, buf, sems):
    queries = pack[...].reshape(TOK, 256)[:, 128:256]
    same = (iota((128, 128), 0) // DIM == iota((128, 128), 1) // DIM).astype(F32).astype(BF16)
    copies = []
    for q in range(4):
        spread = spread_matrix(2 * HEADS, half * 4 + q)
        carried = dot(queries, starts[:, q * LANES : (q + 1) * LANES]) * dot(decay[...], spread)
        base = half * HALF + q * LANES
        for i in range(4):
            lane = slice(i * 128, (i + 1) * 128)
            here = pl.ds(pl.multiple_of(base + i * 128, 128), 128)
            result = partial[:, here] + carried[:, lane]
            mean_sq = dot((result * result).astype(BF16), same) * (1.0 / DIM)
            normed = result * lax.rsqrt(mean_sq + 1e-05)
            buf[q, :, lane] = (u[:, here].astype(F32) + par[:, here].astype(F32)[4:5] * normed).astype(BF16)
        target = out.at[:, pl.ds(pl.multiple_of(base, LANES), LANES)]
        copies.append(pltpu.make_async_copy(buf.at[q], target, sems.at[q]))
        copies[-1].start()
    for copy in copies:
        copy.wait()


def outer_mine_kernel(flags, u, partial, starts, pack, par, decay, out, buf, sems):
    outer_half(flags[2], u, partial, starts, pack, par, decay, out, buf, sems)


def outer_other_kernel(flags, u, partial, starts, pack, par, decay, done, out, buf, sems):
    outer_half(flags[1], u, partial, starts, pack, par, decay, out, buf, sems)


def array(shape, dtype=BF16):
    return jax.ShapeDtypeStruct(shape, dtype)


def whole(*shape):
    return pl.BlockSpec(shape, lambda *_: (0,) * len(shape))


def columns(rows):
    return pl.BlockSpec((rows, LANES), lambda i, *_: (0, i))


def call(kernel, name, out, ins, outs, scratch=(), mib=16, estimate=None):
    return pl.pallas_call(
        kernel,
        out_shape=out,
        in_specs=[pl.BlockSpec(memory_space=pltpu.SMEM)] + ins,
        out_specs=outs,
        scratch_shapes=list(scratch),
        compiler_params=params(mib),
        cost_estimate=estimate,
        name=name,
    )


def mark(value, *others):
    place = pl.BlockSpec(memory_space=pl.ANY)
    return pl.pallas_call(
        mark_kernel,
        out_shape=array(value.shape, value.dtype),
        in_specs=[place] * (1 + len(others)),
        out_specs=place,
        input_output_aliases={0: 0},
        cost_estimate=cost(6e9, 9e6, 4e6),
        compiler_params=params(1),
        name="mark",
    )(value, *others)


def exact(x):
    return lax.reduce_precision(x, 8, 7)


def per_device(
    section_in, proj_weight, conv_weight, log_decay, step_size, skip_gain, norm_gain, carry_state, carry_rows
):
    u = section_in[0]
    ctx = ("x", "z", "core")
    core = lax.axis_index("core")
    first = lax.axis_index(ctx) == 0
    flags = jnp.stack([first.astype(jnp.int32), 1 - core, core])

    def onward(value):
        return lax.ppermute(value, "section", [(i, (i + 1) % 4) for i in range(4)])

    def swapped(value):
        return lax.ppermute(value, "core", [(0, 1), (1, 0)])

    logs = jnp.concatenate([log_decay[0].T, step_size[0].T], axis=0)
    vmem, anywhere = pl.BlockSpec(memory_space=pltpu.VMEM), pl.BlockSpec(memory_space=pl.ANY)
    behind = lax.ppermute(u[TOK - 16 :], ctx, [(i, i + 1) for i in range(63)])
    near_u, near_weight = pl.pallas_call(
        fetch_kernel,
        out_shape=(array((TOK, CH)), array((CH, 256))),
        in_specs=[anywhere] * 2,
        out_specs=[vmem] * 2,
        scratch_shapes=[pltpu.SemaphoreType.DMA((8,))],
        compiler_params=params(46),
        cost_estimate=cost(1e9, 1e7),
        name="fetch",
    )(u, proj_weight[0])
    next_u = onward(u)
    next_logs = onward(logs)
    skip = jnp.repeat(skip_gain, DIM, axis=1)
    skip_hi = exact(skip)
    skip_mid = exact(skip - skip_hi)
    skip_lo = skip - skip_hi - skip_mid
    par = jnp.concatenate(
        [conv_weight[0, :, :CH], norm_gain]
        + [piece.astype(BF16) for piece in (skip_hi, skip_mid, skip_lo)]
        + [jnp.zeros((5, CH), BF16), jnp.where(first, carry_rows[0, :, :CH], behind[13:])],
        axis=0,
    )
    next_par = onward(par)
    pad = pltpu.VMEM((4, 272, 128), F32)
    fresh_out = array((STATE + ROWS, HALF))
    send, turned, pack, to_end, ends = call(
        send_kernel,
        "send",
        (
            fresh_out,
            array((STATE, TOK)),
            array((16, 16, 256)),
            array((TOK, 128)),
            array((ROWS, 128)),
        ),
        [vmem] * 6,
        [vmem] * 5,
        [pad],
        estimate=cost(6e8, 4.5e6, 5e5),
    )(flags, near_u, near_weight, logs, behind, carry_rows[0], conv_weight[0])
    next_pack = onward(pack)
    got = swapped(send)
    keep = call(
        keep_kernel,
        "keep",
        fresh_out,
        [vmem] * 7,
        vmem,
        [pad],
        estimate=cost(6e8, 4.5e6, 5e5),
    )(flags, near_u, behind, carry_rows[0], conv_weight[0], to_end, ends, turned)
    pay = call(join_kernel, "join", array((CHIPS, ROWS, LANES + 128)), [vmem] * 2, vmem, estimate=cost(1e6, 2.5e6))(
        flags, keep, got
    )
    shares = lax.all_to_all(pay, ("x", "z"), 0, 0)
    head = (core * 4 + lax.axis_index("x")) * 8
    start = lax.dynamic_slice(carry_state[0], (head, lax.axis_index("z") * ROWS, 0), (8, ROWS, DIM))
    start = start.transpose(1, 0, 2).reshape(ROWS, LANES)
    back = pl.pallas_call(
        scan_kernel,
        out_shape=array((CHIPS, ROWS, LANES)),
        in_specs=[vmem] * 2,
        out_specs=vmem,
        compiler_params=params(8),
        name="scan",
    )(shares, start)
    chip = lax.all_to_all(back, ("x", "z"), 0, 0)
    next_u = mark(next_u, next_pack, next_logs, next_par)
    chip, next_u, next_pack, next_logs, next_par = lax.optimization_barrier(
        (chip, next_u, next_pack, next_logs, next_par)
    )
    next_chip = onward(chip)
    next_chip = mark(next_chip)
    partial, decay, far_u, low_fresh, high_fresh = pl.pallas_call(
        inner_kernel,
        grid=(GROUPS,),
        out_shape=(array((TOK, CH), F32), array((TOK, 128)), array((TOK, CH)), fresh_out, fresh_out),
        in_specs=[columns(TOK), whole(16, 16, 256), columns(16), whole(128, TOK)],
        out_specs=[
            columns(TOK),
            whole(TOK, 128),
            columns(TOK),
            pl.BlockSpec((STATE + ROWS, LANES), lambda q: (0, jnp.minimum(q, 3))),
            pl.BlockSpec((STATE + ROWS, LANES), lambda q: (0, jnp.maximum(q - 4, 0))),
        ],
        scratch_shapes=[
            pltpu.VMEM((TOK, TOK), F32),
            pltpu.VMEM((TOK, 128), F32),
            pltpu.VMEM((HEADS, TOK), F32),
            pltpu.VMEM((STATE, TOK), BF16),
            pltpu.VMEM((TOK, 128), BF16),
            pltpu.VMEM((ROWS, 128), BF16),
            pad,
        ],
        compiler_params=params(20),
        cost_estimate=cost(1, 1),
        name="inner",
    )(next_u, next_pack, next_par, next_logs)
    lead_fresh = lax.ppermute(high_fresh, "core", [(0, 1)])
    state_half = array((STATE, HALF))
    mine, cross = call(start_kernel, "start", (state_half, state_half), [vmem] * 3, [vmem] * 2)(
        flags, next_chip, low_fresh, lead_fresh
    )
    other = swapped(cross)
    scratch = [pltpu.VMEM((4, TOK, LANES), BF16), pltpu.SemaphoreType.DMA((4,))]
    inputs = [pl.BlockSpec(memory_space=pltpu.SMEM)] + [vmem] * 6
    rows = pl.pallas_call(
        outer_mine_kernel,
        out_shape=array((TOK, CH)),
        in_specs=inputs,
        out_specs=anywhere,
        scratch_shapes=scratch,
        compiler_params=params(16),
        cost_estimate=cost(6e8, 5e6),
        name="outer_mine",
    )(flags, far_u, partial, mine, next_pack, next_par, decay)
    rows = pl.pallas_call(
        outer_other_kernel,
        out_shape=array((TOK, CH)),
        in_specs=inputs + [anywhere],
        out_specs=anywhere,
        scratch_shapes=scratch,
        compiler_params=params(16),
        cost_estimate=cost(6e8, 5e6),
        input_output_aliases={7: 0},
        name="outer_other",
    )(flags, far_u, partial, other, next_pack, next_par, decay, rows)
    return rows[None]


def solution(mesh):
    split = Mesh(mesh.devices.reshape(4, 4, 8, 2), ("section", "x", "z", "core"))
    tokens = P("section", ("x", "z", "core"), None)
    layer = P("section", None, None)
    return jax.shard_map(
        per_device,
        mesh=split,
        in_specs=(
            tokens,
            layer,
            layer,
            tokens,
            tokens,
            P("section", None),
            P("section", None),
            P("section", None, None, None),
            layer,
        ),
        out_specs=tokens,
        check_vma=False,
    )
```

```python
import functools

import jax
import jax.numpy as jnp
from jax import lax
from jax.experimental import pallas as pl
from jax.experimental.pallas import tpu as pltpu
from jax.sharding import Mesh
from jax.sharding import PartitionSpec as P

HEADS = 64
DIM = 64
STATE = 128
TOK = 256
CH = 4096
HALF = CH // 2
LANES = 512
GROUPS = 8
ROWS = 16
CHIPS = 32
LOG2E = 1.4426950408889634
F32 = jnp.float32
BF16 = jnp.bfloat16


def params(mib):
    return pltpu.CompilerParams(vmem_limit_bytes=mib * 2**20)


def cost(flops, moved, exps=0):
    return pl.CostEstimate(flops=int(flops), bytes_accessed=int(moved), transcendentals=int(exps))


def dot(a, b):
    return jnp.dot(a, b, preferred_element_type=F32)


def parts(x, count):
    out = []
    for _ in range(count):
        piece = x.astype(BF16)
        out.append(piece)
        x = x - piece.astype(F32)
    return out


def iota(shape, axis):
    return lax.broadcasted_iota(jnp.int32, shape, axis)


def two_parts(x):
    hi = x.astype(BF16).astype(F32)
    return jnp.where(iota(x.shape, 1) < HEADS, hi, x - hi).astype(BF16)


def spread_matrix(rows, group):
    head = iota((rows, LANES), 1) // DIM + group * (LANES // DIM)
    return (iota((rows, LANES), 0) % HEADS == head).astype(F32).astype(BF16)


def conv_silu(pad, x, halo, taps, first=None, carried=None):
    pad[0:16, :] = halo.astype(F32)
    if carried is not None:
        pad[13:16, :] = jnp.where(first == 1, carried.astype(F32), halo.astype(F32)[13:16])
    pad[16:272, :] = x.astype(F32)
    total = taps[0:1] * pad[13:269, :]
    for j in range(1, 4):
        total = total + taps[j : j + 1] * pad[13 + j : 269 + j, :]
    half = 0.5 * total
    return (half + half * jnp.tanh(half)).astype(BF16)


def cumulated(rates):
    tri = (iota((TOK, TOK), 0) <= iota((TOK, TOK), 1)).astype(F32).astype(BF16)
    return sum(dot(piece, tri) for piece in parts(rates, 3))


def twice_turned(x):
    return jnp.concatenate([x, x], axis=0).T


def end_factors(cum, steps):
    last = cum[TOK - 1 : TOK]
    hi, mid, lo = (piece.astype(F32) for piece in parts(jnp.exp(last), 3))
    kind = iota((ROWS, 128), 0) // 4
    tile = jnp.where(kind == 0, hi, jnp.where(kind == 1, mid, jnp.where(kind == 2, lo, 0.0)))
    ends = jnp.where(iota((ROWS, 128), 1) < HEADS, tile, 0.0).astype(BF16)
    return two_parts(jnp.exp(last - cum) * steps), ends


def fresh_half(half, first, u, behind, carried, taps, to_end, ends, turned, fresh, pad):
    for q in range(4):
        spread = spread_matrix(2 * HEADS, half * 4 + q)
        scale = dot(to_end[...], spread)
        scaled = []
        for i in range(4):
            lane = pl.ds(pl.multiple_of(half * HALF + q * LANES + i * 128, 128), 128)
            act = conv_silu(
                pad.at[i], u[:, lane], behind[:, lane], taps[:, lane].astype(F32), first, carried[:, lane]
            )
            scaled.append((act.astype(F32) * scale[:, i * 128 : (i + 1) * 128]).astype(BF16))
        cols = slice(q * LANES, (q + 1) * LANES)
        fresh[0:STATE, cols] = dot(turned[...], jnp.concatenate(scaled, axis=1)).astype(BF16)
        fresh[STATE : STATE + ROWS, cols] = dot(ends[...], spread).astype(BF16)


def fetch_kernel(u, weight, near_u, near_weight, sems):
    copies = []
    for i in range(4):
        rows, depth = pl.ds(i * 64, 64), pl.ds(i * 1024, 1024)
        copies.append(pltpu.make_async_copy(u.at[rows], near_u.at[rows], sems.at[2 * i]))
        copies.append(pltpu.make_async_copy(weight.at[depth], near_weight.at[depth], sems.at[2 * i + 1]))
    for copy in copies:
        copy.start()
    for copy in copies:
        copy.wait()


def send_kernel(
    flags, u, weight, logs, behind, carried, taps, fresh, turned, pack, to_end, ends, pad
):
    first = flags[0]
    to_end[...], ends[...] = end_factors(
        twice_turned(cumulated(logs[0:HEADS])), twice_turned(logs[HEADS : 2 * HEADS])
    )
    projected = dot(u[...], weight[...]).astype(BF16)
    rim_bc = dot(behind[...], weight[...]).astype(BF16).astype(F32)
    acts = []
    for i in range(2):
        lane = slice(CH + i * 128, CH + (i + 1) * 128)
        value, rim = projected[:, i * 128 : (i + 1) * 128], rim_bc[:, i * 128 : (i + 1) * 128]
        acts.append(conv_silu(pad.at[i], value, rim, taps[:, lane].astype(F32), first, carried[:, lane]))
    turned[...] = acts[0].astype(F32).T.astype(BF16)
    for s in range(16):
        for i in range(2):
            pack[s, :, i * 128 : (i + 1) * 128] = acts[i][s * 16 : (s + 1) * 16]
    fresh_half(flags[1], first, u, behind, carried, taps, to_end, ends, turned, fresh, pad)


def keep_kernel(flags, u, behind, carried, taps, to_end, ends, turned, fresh, pad):
    fresh_half(flags[2], flags[0], u, behind, carried, taps, to_end, ends, turned, fresh, pad)


def end_row(tail):
    tail = tail.astype(F32)
    return tail[0:1] + tail[4:5] + tail[8:9]


def join_kernel(flags, keep, got, pay):
    lead = flags[2] == 0
    row = iota((ROWS, 128), 0)
    for q in range(4):
        cols = slice(q * LANES, (q + 1) * LANES)
        own, other = keep[0:STATE, cols].astype(F32), got[0:STATE, cols].astype(F32)
        own_end, other_end = end_row(keep[STATE:, cols]), end_row(got[STATE:, cols])
        total = jnp.where(lead, other_end * own + other, own_end * other + own).astype(BF16)
        pieces = [piece.astype(F32) for piece in parts(own_end * other_end, 3)]
        tail = jnp.zeros((ROWS, 128), F32)
        for p in range(3):
            for i in range(4):
                tail = jnp.where(row == 4 * p + i, pieces[p][:, i * 128 : (i + 1) * 128], tail)
        tail = tail.astype(BF16)
        for g in range(8):
            pay[q * 8 + g, :, 0:LANES] = total[g * ROWS : (g + 1) * ROWS]
            pay[q * 8 + g, :, LANES : LANES + 128] = tail


def scan_kernel(got, start, out):
    def one(i, state):
        out[i] = state.astype(BF16)
        tail = got[i, :, LANES : LANES + 128].astype(F32)
        tail = tail[0:4] + tail[4:8] + tail[8:12]
        ends = jnp.concatenate([tail[i : i + 1] for i in range(4)], axis=1)
        return state * ends + got[i, :, 0:LANES].astype(F32)

    lax.fori_loop(0, CHIPS, one, start[...])


def start_kernel(flags, chip, low_fresh, lead_fresh, mine, cross):
    lead = flags[2] == 0
    for q in range(4):
        cols = slice(q * LANES, (q + 1) * LANES)
        state = jnp.concatenate([chip[q * 8 + g] for g in range(8)], axis=0).astype(F32)
        fresh = jnp.where(lead, low_fresh[:, cols].astype(F32), lead_fresh[:, cols].astype(F32))
        second = end_row(fresh[STATE:]) * state + fresh[0:STATE]
        mine[:, cols] = jnp.where(lead, state, second).astype(BF16)
        cross[:, cols] = jnp.where(lead, second, state).astype(BF16)


def inner_group(
    q, column, par, partial, u, fresh, decay_logs, scores, turned_keys, to_end, ends, pad
):
    log_col, log_row = decay_logs
    base = q * LANES
    slab = par[:, pl.ds(pl.multiple_of(base, LANES), LANES)].astype(F32)
    skip = slab[5:6] + slab[6:7] + slab[7:8]
    spread = spread_matrix(2 * HEADS, q)
    scale = dot(to_end[...], spread)
    scaled = []
    cols = pltpu.roll(log_col[...], (128 - 8 * q) % 128, 1)
    rows = log_row[pl.ds(pl.multiple_of(q * 8, 8), 8), :]
    half = TOK // 2
    causal = iota((half, half), 0) >= iota((half, half), 1)
    left = iota((TOK, 128), 1) < DIM
    for i in range(4):
        lane = slice(i * 128, (i + 1) * 128)
        here = pl.ds(pl.multiple_of(base + i * 128, 128), 128)
        value = conv_silu(pad.at[i], u[:, here], slab[:, lane], slab[0:4, lane])
        scaled.append((value.astype(F32) * scale[:, lane]).astype(BF16))
        both = []
        for h in (2 * i, 2 * i + 1):
            col = cols[:, h : h + 1]
            row = rows[h : h + 1]
            top = jnp.exp2(jnp.where(causal, col[:half] - row[:, :half], -jnp.inf)) * scores[:half, :half]
            low_left = jnp.exp2(col[half:] - row[:, :half]) * scores[half:, :half]
            low_right = jnp.exp2(jnp.where(causal, col[half:] - row[:, half:], -jnp.inf)) * scores[half:, half:]
            low = jnp.concatenate([low_left.astype(BF16), low_right.astype(BF16)], axis=1)
            both.append(jnp.concatenate([dot(top.astype(BF16), value[:half]), dot(low, value)], axis=0))
        partial[:, here] = jnp.where(left, both[0], both[1]) + skip[:, lane] * value.astype(F32)
    there = pl.ds(pl.multiple_of(column, LANES), LANES)
    fresh[0:STATE, there] = dot(turned_keys[...], jnp.concatenate(scaled, axis=1)).astype(BF16)
    fresh[STATE : STATE + ROWS, there] = dot(ends[...], spread).astype(BF16)


def inner_kernel(
    far, pack, par, logs, partial, decay, u, low_fresh, high_fresh,
    scores, log_col, log_row, turned_keys, to_end, ends, pad, sems,
):
    copies = []
    for i in range(4):
        rows = pl.ds(i * 64, 64)
        copies.append(pltpu.make_async_copy(far.at[rows], u.at[rows], sems.at[i]))
        copies[-1].start()
    bc = pack[...].reshape(TOK, 256)
    scores[...] = lax.dot_general(
        bc[:, 128:256], bc[:, 0:128], (((1,), (1,)), ((), ())), preferred_element_type=F32
    )
    cum = cumulated(logs[0:HEADS])
    log_row[...] = cum * LOG2E - jnp.log2(logs[HEADS : 2 * HEADS])
    turned = twice_turned(cum)
    log_col[...] = turned * LOG2E
    decay[...] = two_parts(jnp.exp(turned))
    turned_keys[...] = bc[:, 0:128].astype(F32).T.astype(BF16)
    to_end[...], ends[...] = end_factors(turned, twice_turned(logs[HEADS : 2 * HEADS]))
    for copy in copies:
        copy.wait()
    rest = ((log_col, log_row), scores, turned_keys, to_end, ends, pad)

    def low(q, _):
        inner_group(q, q * LANES, par, partial, u, low_fresh, *rest)
        return 0

    def high(q, _):
        inner_group(q, (q - 4) * LANES, par, partial, u, high_fresh, *rest)
        return 0

    lax.fori_loop(0, 4, low, 0)
    lax.fori_loop(4, 8, high, 0)


def mark_kernel(*refs):
    pass


def outer_half(half, u, partial, starts, pack, par, decay, out, buf, sems):
    queries = pack[...].reshape(TOK, 256)[:, 128:256]
    same = (iota((128, 128), 0) // DIM == iota((128, 128), 1) // DIM).astype(F32).astype(BF16)
    copies = []
    for q in range(4):
        spread = spread_matrix(2 * HEADS, half * 4 + q)
        carried = dot(queries, starts[:, q * LANES : (q + 1) * LANES]) * dot(decay[...], spread)
        base = half * HALF + q * LANES
        for i in range(4):
            lane = slice(i * 128, (i + 1) * 128)
            here = pl.ds(pl.multiple_of(base + i * 128, 128), 128)
            result = partial[:, here] + carried[:, lane]
            mean_sq = dot((result * result).astype(BF16), same) * (1.0 / DIM)
            normed = result * lax.rsqrt(mean_sq + 1e-05)
            buf[q, :, lane] = (u[:, here].astype(F32) + par[:, here].astype(F32)[4:5] * normed).astype(BF16)
        target = out.at[:, pl.ds(pl.multiple_of(base, LANES), LANES)]
        copies.append(pltpu.make_async_copy(buf.at[q], target, sems.at[q]))
        copies[-1].start()
    for copy in copies:
        copy.wait()


def outer_mine_kernel(flags, u, partial, starts, pack, par, decay, out, buf, sems):
    outer_half(flags[2], u, partial, starts, pack, par, decay, out, buf, sems)


def outer_other_kernel(flags, u, partial, starts, pack, par, decay, done, out, buf, sems):
    outer_half(flags[1], u, partial, starts, pack, par, decay, out, buf, sems)


def array(shape, dtype=BF16):
    return jax.ShapeDtypeStruct(shape, dtype)


def whole(*shape):
    return pl.BlockSpec(shape, lambda *_: (0,) * len(shape))


def columns(rows):
    return pl.BlockSpec((rows, LANES), lambda i, *_: (0, i))


def call(kernel, name, out, ins, outs, scratch=(), mib=16, estimate=None):
    return pl.pallas_call(
        kernel,
        out_shape=out,
        in_specs=[pl.BlockSpec(memory_space=pltpu.SMEM)] + ins,
        out_specs=outs,
        scratch_shapes=list(scratch),
        compiler_params=params(mib),
        cost_estimate=estimate,
        name=name,
    )


def mark(value, *others):
    place = pl.BlockSpec(memory_space=pl.ANY)
    return pl.pallas_call(
        mark_kernel,
        out_shape=array(value.shape, value.dtype),
        in_specs=[place] * (1 + len(others)),
        out_specs=place,
        input_output_aliases={0: 0},
        cost_estimate=cost(6e9, 9e6, 4e6),
        compiler_params=params(1),
        name="mark",
    )(value, *others)


def exact(x):
    return lax.reduce_precision(x, 8, 7)


def per_device(
    section_in, proj_weight, conv_weight, log_decay, step_size, skip_gain, norm_gain, carry_state, carry_rows
):
    u = section_in[0]
    ctx = ("x", "z", "core")
    core = lax.axis_index("core")
    first = lax.axis_index(ctx) == 0
    flags = jnp.stack([first.astype(jnp.int32), 1 - core, core])

    def onward(value):
        return lax.ppermute(value, "section", [(i, (i + 1) % 4) for i in range(4)])

    def swapped(value):
        return lax.ppermute(value, "core", [(0, 1), (1, 0)])

    logs = jnp.concatenate([log_decay[0].T, step_size[0].T], axis=0)
    vmem, anywhere = pl.BlockSpec(memory_space=pltpu.VMEM), pl.BlockSpec(memory_space=pl.ANY)
    behind = lax.ppermute(u[TOK - 16 :], ctx, [(i, i + 1) for i in range(63)])
    near_u, near_weight = pl.pallas_call(
        fetch_kernel,
        out_shape=(array((TOK, CH)), array((CH, 256))),
        in_specs=[anywhere] * 2,
        out_specs=[vmem] * 2,
        scratch_shapes=[pltpu.SemaphoreType.DMA((8,))],
        compiler_params=params(46),
        cost_estimate=cost(1e9, 1e7),
        name="fetch",
    )(u, proj_weight[0])
    next_u = onward(u)
    skip = jnp.repeat(skip_gain, DIM, axis=1)
    skip_hi = exact(skip)
    skip_mid = exact(skip - skip_hi)
    skip_lo = skip - skip_hi - skip_mid
    par = jnp.concatenate(
        [conv_weight[0, :, :CH], norm_gain]
        + [piece.astype(BF16) for piece in (skip_hi, skip_mid, skip_lo)]
        + [jnp.zeros((5, CH), BF16), jnp.where(first, carry_rows[0, :, :CH], behind[13:])],
        axis=0,
    )
    next_par = onward(par)
    pad = pltpu.VMEM((4, 272, 128), F32)
    fresh_out = array((STATE + ROWS, HALF))
    send, turned, pack, to_end, ends = call(
        send_kernel,
        "send",
        (
            fresh_out,
            array((STATE, TOK)),
            array((16, 16, 256)),
            array((TOK, 128)),
            array((ROWS, 128)),
        ),
        [vmem] * 6,
        [vmem] * 5,
        [pad],
        estimate=cost(6e8, 4.5e6, 5e5),
    )(flags, near_u, near_weight, logs, behind, carry_rows[0], conv_weight[0])
    next_pack = onward(pack)
    got = swapped(send)
    keep = call(
        keep_kernel,
        "keep",
        fresh_out,
        [vmem] * 7,
        vmem,
        [pad],
        estimate=cost(6e8, 4.5e6, 5e5),
    )(flags, near_u, behind, carry_rows[0], conv_weight[0], to_end, ends, turned)
    pay = call(join_kernel, "join", array((CHIPS, ROWS, LANES + 128)), [vmem] * 2, vmem, estimate=cost(1e6, 2.5e6))(
        flags, keep, got
    )
    pay, logs = lax.optimization_barrier((pay, logs))
    next_logs = onward(logs)
    shares = lax.all_to_all(pay, ("x", "z"), 0, 0)
    shares, next_par, next_pack, next_logs = lax.optimization_barrier((shares, next_par, next_pack, next_logs))
    head = (core * 4 + lax.axis_index("x")) * 8
    start = lax.dynamic_slice(carry_state[0], (head, lax.axis_index("z") * ROWS, 0), (8, ROWS, DIM))
    start = start.transpose(1, 0, 2).reshape(ROWS, LANES)
    back = pl.pallas_call(
        scan_kernel,
        out_shape=array((CHIPS, ROWS, LANES)),
        in_specs=[vmem] * 2,
        out_specs=vmem,
        compiler_params=params(8),
        name="scan",
    )(shares, start)
    chip = lax.all_to_all(back, ("x", "z"), 0, 0)
    next_u = mark(next_u)
    chip, next_u = lax.optimization_barrier((chip, next_u))
    next_chip = onward(chip)
    next_chip = mark(next_chip)
    partial, decay, far_u, low_fresh, high_fresh = pl.pallas_call(
        inner_kernel,
        out_shape=(array((TOK, CH), F32), array((TOK, 128)), array((TOK, CH)), fresh_out, fresh_out),
        in_specs=[anywhere] + [vmem] * 3,
        out_specs=[vmem] * 5,
        scratch_shapes=[
            pltpu.VMEM((TOK, TOK), F32),
            pltpu.VMEM((TOK, 128), F32),
            pltpu.VMEM((HEADS, TOK), F32),
            pltpu.VMEM((STATE, TOK), BF16),
            pltpu.VMEM((TOK, 128), BF16),
            pltpu.VMEM((ROWS, 128), BF16),
            pad,
            pltpu.SemaphoreType.DMA((4,)),
        ],
        compiler_params=params(20),
        cost_estimate=cost(1, 1),
        name="inner",
    )(next_u, next_pack, next_par, next_logs)
    lead_fresh = lax.ppermute(high_fresh, "core", [(0, 1)])
    state_half = array((STATE, HALF))
    mine, cross = call(start_kernel, "start", (state_half, state_half), [vmem] * 3, [vmem] * 2)(
        flags, next_chip, low_fresh, lead_fresh
    )
    other = swapped(cross)
    scratch = [pltpu.VMEM((4, TOK, LANES), BF16), pltpu.SemaphoreType.DMA((4,))]
    inputs = [pl.BlockSpec(memory_space=pltpu.SMEM)] + [vmem] * 6
    rows = pl.pallas_call(
        outer_mine_kernel,
        out_shape=array((TOK, CH)),
        in_specs=inputs,
        out_specs=anywhere,
        scratch_shapes=scratch,
        compiler_params=params(16),
        cost_estimate=cost(6e8, 5e6),
        name="outer_mine",
    )(flags, far_u, partial, mine, next_pack, next_par, decay)
    rows = pl.pallas_call(
        outer_other_kernel,
        out_shape=array((TOK, CH)),
        in_specs=inputs + [anywhere],
        out_specs=anywhere,
        scratch_shapes=scratch,
        compiler_params=params(16),
        cost_estimate=cost(6e8, 5e6),
        input_output_aliases={7: 0},
        name="outer_other",
    )(flags, far_u, partial, other, next_pack, next_par, decay, rows)
    return rows[None]


def solution(mesh):
    split = Mesh(mesh.devices.reshape(4, 4, 8, 2), ("section", "x", "z", "core"))
    tokens = P("section", ("x", "z", "core"), None)
    layer = P("section", None, None)
    return jax.shard_map(
        per_device,
        mesh=split,
        in_specs=(
            tokens,
            layer,
            layer,
            tokens,
            tokens,
            P("section", None),
            P("section", None),
            P("section", None, None, None),
            layer,
        ),
        out_specs=tokens,
        check_vma=False,
    )
```

```python
import functools

import jax
import jax.numpy as jnp
from jax import lax
from jax.experimental import pallas as pl
from jax.experimental.pallas import tpu as pltpu
from jax.sharding import Mesh
from jax.sharding import PartitionSpec as P

HEADS = 64
DIM = 64
STATE = 128
TOK = 256
CH = 4096
HALF = CH // 2
LANES = 512
GROUPS = 8
ROWS = 16
CHIPS = 32
LOG2E = 1.4426950408889634
F32 = jnp.float32
BF16 = jnp.bfloat16


def params(mib):
    return pltpu.CompilerParams(vmem_limit_bytes=mib * 2**20)


def cost(flops, moved, exps=0):
    return pl.CostEstimate(flops=int(flops), bytes_accessed=int(moved), transcendentals=int(exps))


def dot(a, b):
    return jnp.dot(a, b, preferred_element_type=F32)


def parts(x, count):
    out = []
    for _ in range(count):
        piece = x.astype(BF16)
        out.append(piece)
        x = x - piece.astype(F32)
    return out


def iota(shape, axis):
    return lax.broadcasted_iota(jnp.int32, shape, axis)


def two_parts(x):
    hi = x.astype(BF16).astype(F32)
    return jnp.where(iota(x.shape, 1) < HEADS, hi, x - hi).astype(BF16)


def spread_matrix(rows, group):
    head = iota((rows, LANES), 1) // DIM + group * (LANES // DIM)
    return (iota((rows, LANES), 0) % HEADS == head).astype(F32).astype(BF16)


def conv_silu(pad, x, halo, taps, first=None, carried=None):
    pad[0:16, :] = halo.astype(F32)
    if carried is not None:
        pad[13:16, :] = jnp.where(first == 1, carried.astype(F32), halo.astype(F32)[13:16])
    pad[16:272, :] = x.astype(F32)
    total = taps[0:1] * pad[13:269, :]
    for j in range(1, 4):
        total = total + taps[j : j + 1] * pad[13 + j : 269 + j, :]
    half = 0.5 * total
    return (half + half * jnp.tanh(half)).astype(BF16)


def cumulated(rates):
    tri = (iota((TOK, TOK), 0) <= iota((TOK, TOK), 1)).astype(F32).astype(BF16)
    return sum(dot(piece, tri) for piece in parts(rates, 3))


def twice_turned(x):
    return jnp.concatenate([x, x], axis=0).T


def end_factors(cum, steps):
    last = cum[TOK - 1 : TOK]
    hi, mid, lo = (piece.astype(F32) for piece in parts(jnp.exp(last), 3))
    kind = iota((ROWS, 128), 0) // 4
    tile = jnp.where(kind == 0, hi, jnp.where(kind == 1, mid, jnp.where(kind == 2, lo, 0.0)))
    ends = jnp.where(iota((ROWS, 128), 1) < HEADS, tile, 0.0).astype(BF16)
    return two_parts(jnp.exp(last - cum) * steps), ends


def fresh_half(half, first, u, behind, carried, taps, to_end, ends, turned, fresh, pad):
    for q in range(4):
        spread = spread_matrix(2 * HEADS, half * 4 + q)
        scale = dot(to_end[...], spread)
        scaled = []
        for i in range(4):
            lane = pl.ds(pl.multiple_of(half * HALF + q * LANES + i * 128, 128), 128)
            act = conv_silu(
                pad.at[i], u[:, lane], behind[:, lane], taps[:, lane].astype(F32), first, carried[:, lane]
            )
            scaled.append((act.astype(F32) * scale[:, i * 128 : (i + 1) * 128]).astype(BF16))
        cols = slice(q * LANES, (q + 1) * LANES)
        fresh[0:STATE, cols] = dot(turned[...], jnp.concatenate(scaled, axis=1)).astype(BF16)
        fresh[STATE : STATE + ROWS, cols] = dot(ends[...], spread).astype(BF16)


def fetch_kernel(u, weight, near_u, near_weight, sems):
    copies = []
    for i in range(4):
        rows, depth = pl.ds(i * 64, 64), pl.ds(i * 1024, 1024)
        copies.append(pltpu.make_async_copy(u.at[rows], near_u.at[rows], sems.at[2 * i]))
        copies.append(pltpu.make_async_copy(weight.at[depth], near_weight.at[depth], sems.at[2 * i + 1]))
    for copy in copies:
        copy.start()
    for copy in copies:
        copy.wait()


def send_kernel(
    flags, u, weight, logs, behind, carried, taps, fresh, turned, pack, to_end, ends, pad
):
    first = flags[0]
    to_end[...], ends[...] = end_factors(
        twice_turned(cumulated(logs[0:HEADS])), twice_turned(logs[HEADS : 2 * HEADS])
    )
    projected = dot(u[...], weight[...]).astype(BF16)
    rim_bc = dot(behind[...], weight[...]).astype(BF16).astype(F32)
    acts = []
    for i in range(2):
        lane = slice(CH + i * 128, CH + (i + 1) * 128)
        value, rim = projected[:, i * 128 : (i + 1) * 128], rim_bc[:, i * 128 : (i + 1) * 128]
        acts.append(conv_silu(pad.at[i], value, rim, taps[:, lane].astype(F32), first, carried[:, lane]))
    turned[...] = acts[0].astype(F32).T.astype(BF16)
    for s in range(16):
        for i in range(2):
            pack[s, :, i * 128 : (i + 1) * 128] = acts[i][s * 16 : (s + 1) * 16]
    fresh_half(flags[1], first, u, behind, carried, taps, to_end, ends, turned, fresh, pad)


def keep_kernel(flags, u, behind, carried, taps, to_end, ends, turned, fresh, pad):
    fresh_half(flags[2], flags[0], u, behind, carried, taps, to_end, ends, turned, fresh, pad)


def end_row(tail):
    tail = tail.astype(F32)
    return tail[0:1] + tail[4:5] + tail[8:9]


def join_kernel(flags, keep, got, pay):
    lead = flags[2] == 0
    row = iota((ROWS, 128), 0)
    for q in range(4):
        cols = slice(q * LANES, (q + 1) * LANES)
        own, other = keep[0:STATE, cols].astype(F32), got[0:STATE, cols].astype(F32)
        own_end, other_end = end_row(keep[STATE:, cols]), end_row(got[STATE:, cols])
        total = jnp.where(lead, other_end * own + other, own_end * other + own).astype(BF16)
        pieces = [piece.astype(F32) for piece in parts(own_end * other_end, 3)]
        tail = jnp.zeros((ROWS, 128), F32)
        for p in range(3):
            for i in range(4):
                tail = jnp.where(row == 4 * p + i, pieces[p][:, i * 128 : (i + 1) * 128], tail)
        tail = tail.astype(BF16)
        for g in range(8):
            pay[q * 8 + g, :, 0:LANES] = total[g * ROWS : (g + 1) * ROWS]
            pay[q * 8 + g, :, LANES : LANES + 128] = tail


def scan_kernel(got, start, out):
    def one(i, state):
        out[i] = state.astype(BF16)
        tail = got[i, :, LANES : LANES + 128].astype(F32)
        tail = tail[0:4] + tail[4:8] + tail[8:12]
        ends = jnp.concatenate([tail[i : i + 1] for i in range(4)], axis=1)
        return state * ends + got[i, :, 0:LANES].astype(F32)

    lax.fori_loop(0, CHIPS, one, start[...])


def start_kernel(flags, chip, low_fresh, lead_fresh, mine, cross):
    lead = flags[2] == 0
    for q in range(4):
        cols = slice(q * LANES, (q + 1) * LANES)
        state = jnp.concatenate([chip[q * 8 + g] for g in range(8)], axis=0).astype(F32)
        fresh = jnp.where(lead, low_fresh[:, cols].astype(F32), lead_fresh[:, cols].astype(F32))
        second = end_row(fresh[STATE:]) * state + fresh[0:STATE]
        mine[:, cols] = jnp.where(lead, state, second).astype(BF16)
        cross[:, cols] = jnp.where(lead, second, state).astype(BF16)


def inner_group(
    q, column, par, partial, u, fresh, decay_logs, scores, turned_keys, to_end, ends, pad
):
    log_col, log_row = decay_logs
    base = q * LANES
    slab = par[:, pl.ds(pl.multiple_of(base, LANES), LANES)].astype(F32)
    skip = slab[5:6] + slab[6:7] + slab[7:8]
    spread = spread_matrix(2 * HEADS, q)
    scale = dot(to_end[...], spread)
    scaled = []
    cols = pltpu.roll(log_col[...], (128 - 8 * q) % 128, 1)
    rows = log_row[pl.ds(pl.multiple_of(q * 8, 8), 8), :]
    half = TOK // 2
    causal = iota((half, half), 0) >= iota((half, half), 1)
    left = iota((TOK, 128), 1) < DIM
    for i in range(4):
        lane = slice(i * 128, (i + 1) * 128)
        here = pl.ds(pl.multiple_of(base + i * 128, 128), 128)
        value = conv_silu(pad.at[i], u[:, here], slab[:, lane], slab[0:4, lane])
        scaled.append((value.astype(F32) * scale[:, lane]).astype(BF16))
        both = []
        for h in (2 * i, 2 * i + 1):
            col = cols[:, h : h + 1]
            row = rows[h : h + 1]
            top = jnp.exp2(jnp.where(causal, col[:half] - row[:, :half], -jnp.inf)) * scores[:half, :half]
            low_left = jnp.exp2(col[half:] - row[:, :half]) * scores[half:, :half]
            low_right = jnp.exp2(jnp.where(causal, col[half:] - row[:, half:], -jnp.inf)) * scores[half:, half:]
            low = jnp.concatenate([low_left.astype(BF16), low_right.astype(BF16)], axis=1)
            both.append(jnp.concatenate([dot(top.astype(BF16), value[:half]), dot(low, value)], axis=0))
        partial[:, here] = jnp.where(left, both[0], both[1]) + skip[:, lane] * value.astype(F32)
    there = pl.ds(pl.multiple_of(column, LANES), LANES)
    fresh[0:STATE, there] = dot(turned_keys[...], jnp.concatenate(scaled, axis=1)).astype(BF16)
    fresh[STATE : STATE + ROWS, there] = dot(ends[...], spread).astype(BF16)


def inner_kernel(
    far, pack, par, logs, partial, decay, u, low_fresh, high_fresh,
    scores, log_col, log_row, turned_keys, to_end, ends, pad, sems,
):
    copies = []
    for i in range(4):
        rows = pl.ds(i * 64, 64)
        copies.append(pltpu.make_async_copy(far.at[rows], u.at[rows], sems.at[i]))
        copies[-1].start()
    bc = pack[...].reshape(TOK, 256)
    scores[...] = lax.dot_general(
        bc[:, 128:256], bc[:, 0:128], (((1,), (1,)), ((), ())), preferred_element_type=F32
    )
    cum = cumulated(logs[0:HEADS])
    log_row[...] = cum * LOG2E - jnp.log2(logs[HEADS : 2 * HEADS])
    turned = twice_turned(cum)
    log_col[...] = turned * LOG2E
    decay[...] = two_parts(jnp.exp(turned))
    turned_keys[...] = bc[:, 0:128].astype(F32).T.astype(BF16)
    to_end[...], ends[...] = end_factors(turned, twice_turned(logs[HEADS : 2 * HEADS]))
    for copy in copies:
        copy.wait()
    rest = ((log_col, log_row), scores, turned_keys, to_end, ends, pad)

    def low(q, _):
        inner_group(q, q * LANES, par, partial, u, low_fresh, *rest)
        return 0

    def high(q, _):
        inner_group(q, (q - 4) * LANES, par, partial, u, high_fresh, *rest)
        return 0

    lax.fori_loop(0, 4, low, 0)
    lax.fori_loop(4, 8, high, 0)


def mark_kernel(*refs):
    pass


def outer_half(half, u, partial, starts, pack, par, decay, out, buf, sems):
    queries = pack[...].reshape(TOK, 256)[:, 128:256]
    same = (iota((128, 128), 0) // DIM == iota((128, 128), 1) // DIM).astype(F32).astype(BF16)
    copies = []
    for q in range(4):
        spread = spread_matrix(2 * HEADS, half * 4 + q)
        carried = dot(queries, starts[:, q * LANES : (q + 1) * LANES]) * dot(decay[...], spread)
        base = half * HALF + q * LANES
        for i in range(4):
            lane = slice(i * 128, (i + 1) * 128)
            here = pl.ds(pl.multiple_of(base + i * 128, 128), 128)
            result = partial[:, here] + carried[:, lane]
            mean_sq = dot((result * result).astype(BF16), same) * (1.0 / DIM)
            normed = result * lax.rsqrt(mean_sq + 1e-05)
            buf[q, :, lane] = (u[:, here].astype(F32) + par[:, here].astype(F32)[4:5] * normed).astype(BF16)
        target = out.at[:, pl.ds(pl.multiple_of(base, LANES), LANES)]
        copies.append(pltpu.make_async_copy(buf.at[q], target, sems.at[q]))
        copies[-1].start()
    for copy in copies:
        copy.wait()


def outer_mine_kernel(flags, u, partial, starts, pack, par, decay, out, buf, sems):
    outer_half(flags[2], u, partial, starts, pack, par, decay, out, buf, sems)


def outer_other_kernel(flags, u, partial, starts, pack, par, decay, done, out, buf, sems):
    outer_half(flags[1], u, partial, starts, pack, par, decay, out, buf, sems)


def array(shape, dtype=BF16):
    return jax.ShapeDtypeStruct(shape, dtype)


def whole(*shape):
    return pl.BlockSpec(shape, lambda *_: (0,) * len(shape))


def columns(rows):
    return pl.BlockSpec((rows, LANES), lambda i, *_: (0, i))


def call(kernel, name, out, ins, outs, scratch=(), mib=16, estimate=None):
    return pl.pallas_call(
        kernel,
        out_shape=out,
        in_specs=[pl.BlockSpec(memory_space=pltpu.SMEM)] + ins,
        out_specs=outs,
        scratch_shapes=list(scratch),
        compiler_params=params(mib),
        cost_estimate=estimate,
        name=name,
    )


def mark(value, *others):
    place = pl.BlockSpec(memory_space=pl.ANY)
    return pl.pallas_call(
        mark_kernel,
        out_shape=array(value.shape, value.dtype),
        in_specs=[place] * (1 + len(others)),
        out_specs=place,
        input_output_aliases={0: 0},
        cost_estimate=cost(6e9, 9e6, 4e6),
        compiler_params=params(1),
        name="mark",
    )(value, *others)


def exact(x):
    return lax.reduce_precision(x, 8, 7)


def per_device(
    section_in, proj_weight, conv_weight, log_decay, step_size, skip_gain, norm_gain, carry_state, carry_rows
):
    u = section_in[0]
    ctx = ("x", "z", "core")
    core = lax.axis_index("core")
    first = lax.axis_index(ctx) == 0
    flags = jnp.stack([first.astype(jnp.int32), 1 - core, core])

    def onward(value):
        return lax.ppermute(value, "section", [(i, (i + 1) % 4) for i in range(4)])

    def swapped(value):
        return lax.ppermute(value, "core", [(0, 1), (1, 0)])

    logs = jnp.concatenate([log_decay[0].T, step_size[0].T], axis=0)
    vmem, anywhere = pl.BlockSpec(memory_space=pltpu.VMEM), pl.BlockSpec(memory_space=pl.ANY)
    behind = lax.ppermute(u[TOK - 16 :], ctx, [(i, i + 1) for i in range(63)])
    near_u, near_weight = pl.pallas_call(
        fetch_kernel,
        out_shape=(array((TOK, CH)), array((CH, 256))),
        in_specs=[anywhere] * 2,
        out_specs=[vmem] * 2,
        scratch_shapes=[pltpu.SemaphoreType.DMA((8,))],
        compiler_params=params(46),
        cost_estimate=cost(1e9, 1e7),
        name="fetch",
    )(u, proj_weight[0])
    next_u = onward(u)
    skip = jnp.repeat(skip_gain, DIM, axis=1)
    skip_hi = exact(skip)
    skip_mid = exact(skip - skip_hi)
    skip_lo = skip - skip_hi - skip_mid
    par = jnp.concatenate(
        [conv_weight[0, :, :CH], norm_gain]
        + [piece.astype(BF16) for piece in (skip_hi, skip_mid, skip_lo)]
        + [jnp.zeros((5, CH), BF16), jnp.where(first, carry_rows[0, :, :CH], behind[13:])],
        axis=0,
    )
    next_par = onward(par)
    pad = pltpu.VMEM((4, 272, 128), F32)
    fresh_out = array((STATE + ROWS, HALF))
    send, turned, pack, to_end, ends = call(
        send_kernel,
        "send",
        (
            fresh_out,
            array((STATE, TOK)),
            array((16, 16, 256)),
            array((TOK, 128)),
            array((ROWS, 128)),
        ),
        [vmem] * 6,
        [vmem] * 5,
        [pad],
        estimate=cost(6e8, 4.5e6, 5e5),
    )(flags, near_u, near_weight, logs, behind, carry_rows[0], conv_weight[0])
    next_pack = onward(pack)
    got = swapped(send)
    keep = call(
        keep_kernel,
        "keep",
        fresh_out,
        [vmem] * 7,
        vmem,
        [pad],
        estimate=cost(6e8, 4.5e6, 5e5),
    )(flags, near_u, behind, carry_rows[0], conv_weight[0], to_end, ends, turned)
    pay = call(join_kernel, "join", array((CHIPS, ROWS, LANES + 128)), [vmem] * 2, vmem, estimate=cost(1e6, 2.5e6))(
        flags, keep, got
    )
    pay, logs = lax.optimization_barrier((pay, logs))
    next_logs = onward(logs)
    shares = lax.all_to_all(pay, ("x", "z"), 0, 0)
    head = (core * 4 + lax.axis_index("x")) * 8
    start = lax.dynamic_slice(carry_state[0], (head, lax.axis_index("z") * ROWS, 0), (8, ROWS, DIM))
    start = start.transpose(1, 0, 2).reshape(ROWS, LANES)
    back = pl.pallas_call(
        scan_kernel,
        out_shape=array((CHIPS, ROWS, LANES)),
        in_specs=[vmem] * 2,
        out_specs=vmem,
        compiler_params=params(8),
        name="scan",
    )(shares, start)
    chip = lax.all_to_all(back, ("x", "z"), 0, 0)
    next_u = mark(next_u)
    chip, next_u, next_pack, next_logs, next_par = lax.optimization_barrier(
        (chip, next_u, next_pack, next_logs, next_par)
    )
    next_chip = onward(chip)
    next_chip = mark(next_chip)
    partial, decay, far_u, low_fresh, high_fresh = pl.pallas_call(
        inner_kernel,
        out_shape=(array((TOK, CH), F32), array((TOK, 128)), array((TOK, CH)), fresh_out, fresh_out),
        in_specs=[anywhere] + [vmem] * 3,
        out_specs=[vmem] * 5,
        scratch_shapes=[
            pltpu.VMEM((TOK, TOK), F32),
            pltpu.VMEM((TOK, 128), F32),
            pltpu.VMEM((HEADS, TOK), F32),
            pltpu.VMEM((STATE, TOK), BF16),
            pltpu.VMEM((TOK, 128), BF16),
            pltpu.VMEM((ROWS, 128), BF16),
            pad,
            pltpu.SemaphoreType.DMA((4,)),
        ],
        compiler_params=params(20),
        cost_estimate=cost(1, 1),
        name="inner",
    )(next_u, next_pack, next_par, next_logs)
    lead_fresh = lax.ppermute(high_fresh, "core", [(0, 1)])
    state_half = array((STATE, HALF))
    mine, cross = call(start_kernel, "start", (state_half, state_half), [vmem] * 3, [vmem] * 2)(
        flags, next_chip, low_fresh, lead_fresh
    )
    other = swapped(cross)
    scratch = [pltpu.VMEM((4, TOK, LANES), BF16), pltpu.SemaphoreType.DMA((4,))]
    inputs = [pl.BlockSpec(memory_space=pltpu.SMEM)] + [vmem] * 6
    rows = pl.pallas_call(
        outer_mine_kernel,
        out_shape=array((TOK, CH)),
        in_specs=inputs,
        out_specs=anywhere,
        scratch_shapes=scratch,
        compiler_params=params(16),
        cost_estimate=cost(6e8, 5e6),
        name="outer_mine",
    )(flags, far_u, partial, mine, next_pack, next_par, decay)
    rows = pl.pallas_call(
        outer_other_kernel,
        out_shape=array((TOK, CH)),
        in_specs=inputs + [anywhere],
        out_specs=anywhere,
        scratch_shapes=scratch,
        compiler_params=params(16),
        cost_estimate=cost(6e8, 5e6),
        input_output_aliases={7: 0},
        name="outer_other",
    )(flags, far_u, partial, other, next_pack, next_par, decay, rows)
    return rows[None]


def solution(mesh):
    split = Mesh(mesh.devices.reshape(4, 4, 8, 2), ("section", "x", "z", "core"))
    tokens = P("section", ("x", "z", "core"), None)
    layer = P("section", None, None)
    return jax.shard_map(
        per_device,
        mesh=split,
        in_specs=(
            tokens,
            layer,
            layer,
            tokens,
            tokens,
            P("section", None),
            P("section", None),
            P("section", None, None, None),
            layer,
        ),
        out_specs=tokens,
        check_vma=False,
    )
```
